256 devices in a mesh: tm: 4 (over z_lo, core), cam: 64 (over y, x, z_hi).
Axes of the slice: x: 4, y: 4, z: 8 (z_hi: 4, z_lo: 2; z = z_hi * 2 + z_lo), core: 2. Of those that a mesh axis runs over, the one named last changes fastest.
Arguments:
- queries: bfloat16 [8, 64, 128, 1024], P('tm', 'cam'), may hold values from -170 to 170
- key_vectors: bfloat16 [8, 64, 128, 1024], P('tm', 'cam'), may hold values from -6 to 6
- value_vectors: bfloat16 [8, 64, 128, 1024], P('tm', 'cam'), may hold values from -6 to 6
- w_out: bfloat16 [1024, 1024], replicated, may hold values from -0.1875 to 0.1875
- rig_tiles: int32 [64, 7], replicated, may hold values from 0 to 63, as said below
- rig_count: int32 [64], replicated, may hold values from 1 to 7, as said below
- strip_rows: int32 [64, 16], replicated, may hold values from 0 to 127, as said below
- cotangent: bfloat16 [8, 64, 128, 1024], P('tm', 'cam'), may hold values from -6 to 6
Outputs:
- mixed: bfloat16 [8, 64, 128, 1024], P('tm', 'cam')
- grad_queries: bfloat16 [8, 64, 128, 1024], P('tm', 'cam')
- grad_keys: bfloat16 [8, 64, 128, 1024], P('tm', 'cam')
- grad_values: bfloat16 [8, 64, 128, 1024], P('tm', 'cam')
- grad_w_out: float32 [1024, 1024], P(('tm', 'cam'))
The draws below stay inside these ranges and needn't reach their ends.
Inputs may be any that keep to these rules, and one draw needn't show every extreme that they name: `rig_tiles`: row c names 7 different camera-tiles, none of them c. `rig_count`: some camera-tile uses all 7 slots. `strip_rows`: each row holds 16 different token indices.
All inputs are finite; a program needn't handle non-finite values.
Results may differ from the reference program's by a relative error of at most 0.03.
Values may be sent and summed in bfloat16 or wider, within the bound.
No kernel may reach another device: no remote copies, remote signals or barrier semaphores. Data moves between devices by JAX's collectives and lax.ppermute only.
A program may use at most 192 MiB of HBM per device.

```python
import jax
import jax.numpy as jnp
from jax import lax

D = 1024
HEADS = 16
TILE = 128
STRIP = 16
NB = 7
FRAMES = 8
CAMTILES = 64


def keys_shared(key):
    base_keys = jax.random.normal(key, (FRAMES, CAMTILES, TILE, D), jnp.float32)
    return jnp.clip(base_keys, -6.0, 6.0)


def draw_key_vectors(key, part):
    base_keys = keys_shared(key)
    return base_keys.astype(jnp.bfloat16)


def draw_queries(key, part):
    key = jax.random.fold_in(key, 7)
    shape = (FRAMES, CAMTILES, TILE, D)
    fresh_draw = jnp.clip(jax.random.normal(key, shape, jnp.float32), -6.0, 6.0)
    return fresh_draw.astype(jnp.bfloat16)


def draw_rig_tiles(key, part):
    key = jax.random.fold_in(key, 3)
    row_keys = jax.random.split(key, CAMTILES)
    offsets = jax.vmap(lambda row_key: jax.random.permutation(row_key, CAMTILES - 1)[:NB])(row_keys)
    rows = jnp.arange(CAMTILES, dtype=jnp.int32)[:, None]
    return ((rows + 1 + offsets) % CAMTILES).astype(jnp.int32)


def draw_rig_count(key, part):
    key = jax.random.fold_in(key, 5)
    counts = jax.random.randint(key, (CAMTILES,), 1, NB + 1)
    fullest = jax.random.randint(jax.random.fold_in(key, 1), (), 0, CAMTILES)
    return counts.at[fullest].set(NB).astype(jnp.int32)


def draw_strip_rows(key, part):
    key = jax.random.fold_in(key, 9)
    row_keys = jax.random.split(key, CAMTILES)
    picked = jax.vmap(lambda row_key: jax.random.permutation(row_key, TILE)[:STRIP])(row_keys)
    return picked.astype(jnp.int32)


def steps_of(rng, dims, cuts, low, top_value):
    loudness = 1.0
    for dim, shards_of in cuts:
        draws = jax.random.uniform(jax.random.fold_in(jax.random.fold_in(rng, 6), dim), (shards_of,), jnp.float32, low / len(cuts), top_value / len(cuts))
        loudness = loudness * jnp.repeat(jnp.exp(draws), dims[dim] // shards_of).reshape((-1,) + (1,) * (len(dims) - 1 - dim))
    return loudness


def scatter_about(key, extent, spread, limit, cuts=(), kind=jnp.bfloat16):
    factor_of = steps_of(key, extent, cuts, -0.22, 0.18) if cuts else 1.0
    drawn = jax.random.normal(key, extent, jnp.float32) * spread * factor_of
    return jnp.minimum(jnp.maximum(drawn, -limit), limit).astype(kind)


def setup_inputs(seed: int = 0) -> dict:
    splits = jax.random.split(jax.random.key(seed), 9)
    queries = draw_queries(jax.random.fold_in(splits[8], 71), 0)
    key_vectors = draw_key_vectors(jax.random.fold_in(splits[8], 71), 0)
    value_vectors = scatter_about(splits[2], (FRAMES, CAMTILES, TILE, D), 1.0, 6.0, ((0, 4), (1, 64)))
    w_out = scatter_about(splits[3], (D, D), D ** -0.5, 0.1875)
    rig_tiles = draw_rig_tiles(jax.random.fold_in(splits[8], 71), 0)
    rig_count = draw_rig_count(jax.random.fold_in(splits[8], 71), 0)
    strip_rows = draw_strip_rows(jax.random.fold_in(splits[8], 71), 0)
    cotangent = scatter_about(splits[7], (FRAMES, CAMTILES, TILE, D), 1.0, 6.0, ((0, 4), (1, 64)))
    return {"queries": queries, "key_vectors": key_vectors, "value_vectors": value_vectors, "w_out": w_out, "rig_tiles": rig_tiles, "rig_count": rig_count, "strip_rows": strip_rows, "cotangent": cotangent}


def split_heads(tensor):
    return tensor.reshape(tensor.shape[:-1] + (HEADS, tensor.shape[-1] // HEADS))


def masked_scores(query_rows, ctx_keys, visible):
    score_scale = (query_rows.shape[-1] // HEADS) ** -0.5
    scores = jnp.einsum("bqhd,bkhd->bhqk", split_heads(query_rows).astype(jnp.float32), split_heads(ctx_keys).astype(jnp.float32)) * score_scale
    return jnp.where(visible[:, None, None, :], scores, -1e30)


def attend(query_rows, ctx_keys, ctx_vals, visible):
    scores = masked_scores(query_rows, ctx_keys, visible)
    row_max = jnp.max(scores, -1)
    expo = jnp.exp(scores - row_max[..., None])
    row_sum = jnp.sum(expo, -1)
    softmax_prob = expo / row_sum[..., None]
    weights = lax.optimization_barrier(softmax_prob.astype(jnp.bfloat16)).astype(jnp.float32)
    attended = jnp.einsum("bhqk,bkhd->bqhd", weights, split_heads(ctx_vals).astype(jnp.float32))
    return attended.reshape(query_rows.shape).astype(jnp.bfloat16), row_max, row_sum


def delta_of(attended, grad_attended):
    product = split_heads(attended).astype(jnp.float32) * split_heads(grad_attended).astype(jnp.float32)
    return jnp.swapaxes(jnp.sum(product, -1), 1, 2)


def attend_back(query_rows, ctx_keys, ctx_vals, visible, grad_attended, row_max, row_sum, row_delta):
    score_scale = (query_rows.shape[-1] // HEADS) ** -0.5
    scores = masked_scores(query_rows, ctx_keys, visible)
    softmax_prob = jnp.exp(scores - row_max[..., None]) / row_sum[..., None]
    weights = lax.optimization_barrier(softmax_prob.astype(jnp.bfloat16)).astype(jnp.float32)
    grad_heads = split_heads(grad_attended).astype(jnp.float32)
    grad_prob = jnp.einsum("bqhd,bkhd->bhqk", grad_heads, split_heads(ctx_vals).astype(jnp.float32))
    grad_score = (softmax_prob * (grad_prob - row_delta[..., None]) * score_scale).astype(jnp.bfloat16)
    grad_score = lax.optimization_barrier(grad_score).astype(jnp.float32)
    grad_q = jnp.einsum("bhqk,bkhd->bqhd", grad_score, split_heads(ctx_keys).astype(jnp.float32)).reshape(query_rows.shape)
    grad_k = jnp.einsum("bhqk,bqhd->bkhd", grad_score, split_heads(query_rows).astype(jnp.float32)).reshape(ctx_keys.shape)
    grad_v = jnp.einsum("bhqk,bqhd->bkhd", weights, grad_heads).reshape(ctx_keys.shape)
    return grad_q, grad_k, grad_v


def reference(queries, key_vectors, value_vectors, w_out, rig_tiles, rig_count, strip_rows, cotangent):
    frames, tiles, tile_len, model_width = queries.shape
    slot_count = rig_tiles.shape[1]
    strip_len = strip_rows.shape[1]
    key_value = jnp.concatenate([key_vectors, value_vectors], -1)
    tile_ids = jnp.arange(tiles, dtype=jnp.int32)[:, None]
    strips_all = key_value[:, tile_ids, strip_rows]
    chosen_all = strips_all[:, rig_tiles].reshape(frames, tiles, slot_count * strip_len, 2 * model_width)
    slot_visible = jnp.repeat(jnp.arange(slot_count, dtype=jnp.int32)[None, :] < rig_count[:, None], strip_len, axis=1)
    target_tiles = jnp.broadcast_to(rig_tiles[:, :, None], (tiles, slot_count, strip_len))
    target_rows = strip_rows[rig_tiles]

    def one_frame(carry, frame_index):
        kv_grad, weight_grad = carry
        earlier_index = jnp.maximum(frame_index - 1, 0)
        context = jnp.concatenate([key_value[frame_index], key_value[earlier_index], chosen_all[frame_index]], 1)
        visible = jnp.concatenate([jnp.ones((tiles, tile_len), bool), jnp.broadcast_to(frame_index > 0, (tiles, tile_len)), slot_visible], 1)
        ctx_keys = context[..., :model_width]
        ctx_vals = context[..., model_width:]
        query_rows = queries[frame_index]
        attended, row_max, row_sum = attend(query_rows, ctx_keys, ctx_vals, visible)
        flat = attended.reshape(-1, model_width)
        mixed = jnp.dot(flat, w_out, preferred_element_type=jnp.float32).astype(jnp.bfloat16).reshape(tiles, tile_len, model_width)
        grad_flat = cotangent[frame_index].reshape(-1, model_width)
        grad_attended = lax.dot_general(grad_flat, w_out, (((1,), (1,)), ((), ())), preferred_element_type=jnp.float32)
        grad_attended = grad_attended.astype(jnp.bfloat16).reshape(tiles, tile_len, model_width)
        weight_grad = weight_grad + lax.dot_general(flat, grad_flat, (((0,), (0,)), ((), ())), preferred_element_type=jnp.float32)
        row_delta = delta_of(attended, grad_attended)
        grad_q, grad_k, grad_v = attend_back(query_rows, ctx_keys, ctx_vals, visible, grad_attended, row_max, row_sum, row_delta)
        grad_ctx = jnp.concatenate([grad_k, grad_v], -1)
        kv_grad = kv_grad.at[frame_index].add(grad_ctx[:, :tile_len])
        kv_grad = kv_grad.at[earlier_index].add(grad_ctx[:, tile_len:2 * tile_len])
        strip_part = grad_ctx[:, 2 * tile_len:].reshape(tiles, slot_count, strip_len, 2 * model_width)
        frame_grad = kv_grad[frame_index].at[target_tiles, target_rows].add(strip_part)
        kv_grad = kv_grad.at[frame_index].set(frame_grad)
        return (kv_grad, weight_grad), (mixed, grad_q.astype(jnp.bfloat16))

    start = (jnp.zeros((frames, tiles, tile_len, 2 * model_width), jnp.float32), jnp.zeros((model_width, model_width), jnp.float32))
    (kv_grad, weight_grad), (mixed, grad_queries) = lax.scan(one_frame, start, jnp.arange(frames, dtype=jnp.int32))
    grad_keys = kv_grad[..., :model_width].astype(jnp.bfloat16)
    grad_values = kv_grad[..., model_width:].astype(jnp.bfloat16)
    return (mixed, grad_queries, grad_keys, grad_values, weight_grad)
```

```python
import functools

import jax
import jax.numpy as jnp
from jax import lax
from jax.experimental import pallas as pl
from jax.experimental.pallas import tpu as pltpu
from jax.sharding import PartitionSpec as P

TILE = 128
D = 1024
PAIRS = 8
RING = 4
GRID = 16
SLOTS = 8
NEG = -1e30
BF = jnp.bfloat16
F32 = jnp.float32
MIB = 1 << 20

CORE, ZLO, TM, Q, CAM, COUNT = range(6)
ORDER = 8


def nt(a, b):
    return lax.dot_general(a, b, (((1,), (1,)), ((), ())), preferred_element_type=F32)


def tn(a, b):
    return lax.dot_general(a, b, (((0,), (0,)), ((), ())), preferred_element_type=F32)


def nn(a, b):
    return jnp.dot(a, b, preferred_element_type=F32)


def iota(shape, dim):
    return lax.broadcasted_iota(jnp.int32, shape, dim)


def call(body, grid, inputs, outputs, limit_mib, flops, nbytes, scalars=1):
    def spec(entry):
        shape, block, index = entry
        if block is None:
            zeros = (0,) * len(shape.shape)
            return pl.BlockSpec(shape.shape, lambda *_: zeros)
        return pl.BlockSpec(block, index)

    return pl.pallas_call(
        body,
        grid_spec=pltpu.PrefetchScalarGridSpec(
            num_scalar_prefetch=scalars,
            grid=grid,
            in_specs=[spec(e) for e in inputs[scalars:]],
            out_specs=[spec(e) for e in outputs],
        ),
        out_shape=[e[0] for e in outputs],
        compiler_params=pltpu.CompilerParams(vmem_limit_bytes=limit_mib * MIB),
        cost_estimate=pl.CostEstimate(flops=flops, bytes_accessed=nbytes, transcendentals=0),
    )(*[e[0] if isinstance(e, tuple) else e for e in inputs])


def like(shape, dtype=BF):
    return jax.ShapeDtypeStruct(shape, dtype)


def strip_target(info, strip_rows, shape, group):
    s = iota(shape, 0) // group
    target = jnp.zeros(shape, jnp.int32)
    for i in range(GRID):
        target = jnp.where(s == i, strip_rows[info[CAM], i], target)
    return target


def extract_body(info, strip_rows, k, v, out, last):
    shape = (GRID * 8, 2 * TILE)
    r, c = iota(shape, 0), iota(shape, 1)
    hit = (strip_target(info, strip_rows, shape, 8) == c % TILE) & ((r // 2) % 2 == c // TILE)
    total = jnp.zeros((GRID * 8, D // 2), F32)
    for part, ref in enumerate((k, v)):
        whole = ref[...].reshape(2 * TILE, D)
        for half in range(2):
            pick = hit & (r % 2 == part) & ((r // 4) % 2 == half)
            total += nn(pick.astype(F32).astype(BF), whole[:, half * 512 : half * 512 + 512])
        last[part] = ref[1]
    out[...] = total.astype(BF)


def stacked(block):
    first = iota(block.shape, 1) < 64
    zero = jnp.zeros_like(block)
    return jnp.concatenate([jnp.where(first, block, zero), jnp.where(first, zero, block)], 0)


def own_half(wide):
    return jnp.concatenate([wide[:64, :TILE], wide[64:, TILE:]], 0)


def spread(row):
    return jnp.concatenate(
        [jnp.broadcast_to(row[:, :TILE], (64, TILE)), jnp.broadcast_to(row[:, TILE:], (64, TILE))],
        0,
    )


def local_body(info, q, k, v, prev, cot, w, g_out, gt_out, m_out, l_out, o_out):
    cots = cot[...].reshape(2 * TILE, D)
    g_out[...] = nt(cots, w[...]).astype(BF).reshape(2, TILE, TILE)
    gt_out[...] = nt(w[...], cots).astype(BF)
    for f in range(2):
        qs = stacked(q[f] * jnp.asarray(0.125, BF))
        before_k, before_v = (prev[0], prev[1]) if f == 0 else (k[0], v[0])
        s1 = nt(k[f], qs)
        s2 = nt(before_k, qs)
        if f == 0:
            s2 = jnp.where(info[TM] > 0, s2, NEG)
        m = jnp.maximum(jnp.max(s1, 0, keepdims=True), jnp.max(s2, 0, keepdims=True))
        p1 = jnp.exp(s1 - m)
        p2 = jnp.exp(s2 - m)
        m_out[0, f] = m[0]
        l_out[0, f] = jnp.sum(p1, 0) + jnp.sum(p2, 0)
        o_out[0, f] = own_half(tn(v[f], p1.astype(BF)) + tn(before_v, p2.astype(BF)))


def strip_body(
    info, q, g, gt, strips, m1, l1, o1, cot,
    att, back, m_out, rl_out, delta_out, dq_out, w_send, w_keep,
):
    weight = jnp.zeros((TILE, D), F32)
    seen = iota((TILE, 2 * TILE), 0) % SLOTS < info[COUNT]
    for f in range(2):
        qs = stacked(q[f] * jnp.asarray(0.125, BF))
        gs = stacked(g[f])
        ks = strips[:, 2 * f].astype(F32).reshape(TILE, TILE).astype(BF)
        vs = strips[:, 2 * f + 1].astype(F32).reshape(TILE, TILE).astype(BF)
        s = jnp.where(seen, nt(ks, qs), NEG)
        m_old = m1[0, f : f + 1]
        m = jnp.maximum(m_old, jnp.max(s, 0, keepdims=True))
        p = jnp.exp(s - m)
        shrink = jnp.exp(m_old - m)
        rl = 1.0 / (l1[0, f : f + 1] * shrink + jnp.sum(p, 0, keepdims=True))
        p = p * rl
        pb = p.astype(BF)
        ot = (o1[0, f] * spread(shrink * rl) + own_half(tn(vs, pb))).astype(BF)
        prod = gt[:, f * TILE : f * TILE + TILE].astype(F32) * ot.astype(F32)
        delta = jnp.concatenate(
            [jnp.sum(prod[:64], 0, keepdims=True), jnp.sum(prod[64:], 0, keepdims=True)], 1
        )
        ds = (p * (nt(vs, gs) - delta)).astype(BF)
        back[:, 2 * f] = nn(ds, qs).reshape(GRID, SLOTS, TILE).astype(BF)
        back[:, 2 * f + 1] = nn(pb, gs).reshape(GRID, SLOTS, TILE).astype(BF)
        dq_out[0, f] = own_half(tn(ks, ds))
        att[f] = ot.astype(F32).T.astype(BF)
        m_out[0, f] = m[0]
        rl_out[0, f] = rl[0]
        delta_out[0, f] = delta[0]
        weight += nn(ot, cot[f])
    step = pl.program_id(0)

    @pl.when(step < 4)
    def _():
        w_send[0] = weight.astype(BF)

    @pl.when(step >= 4)
    def _():
        w_keep[0] = weight.astype(BF)


def back_body(
    info, q, k, v, prev, g, m, rl, delta, dq, att, w,
    gq_out, gk_out, gv_out, ret_out, mixed_out,
):
    mixed_out[...] = nn(att[...].reshape(2 * TILE, D), w[...]).astype(BF).reshape(2, TILE, TILE)
    for f in range(2):
        qs = stacked(q[f] * jnp.asarray(0.125, BF))
        gs = stacked(g[f])
        total = dq[0, f]
        for own in (True, False):
            if own:
                kb, vb = k[f], v[f]
            elif f == 0:
                kb, vb = prev[0], prev[1]
            else:
                kb, vb = k[0], v[0]
            s = nt(kb, qs)
            if not own and f == 0:
                s = jnp.where(info[TM] > 0, s, NEG)
            p = jnp.exp(s - m[0, f : f + 1]) * rl[0, f : f + 1]
            ds = (p * (nt(vb, gs) - delta[0, f : f + 1])).astype(BF)
            dk = nn(ds, qs)
            dv = nn(p.astype(BF), gs)
            total += own_half(tn(kb, ds))
            if own:
                gk_out[f] = dk
                gv_out[f] = dv
            elif f == 0:
                ret_out[0] = dk.astype(BF)
                ret_out[1] = dv.astype(BF)
            else:
                gk_out[0] += dk
                gv_out[0] += dv
        gq_out[f] = (total * 0.125).T.astype(BF)


def select_body(info, rowid, t0, t1, t2, t3, out):
    table = jnp.concatenate([t0[...], t1[...], t2[...], t3[...]], 0)
    shape = (GRID * 4 * SLOTS, RING * GRID * 8)
    r, c = iota(shape, 0), iota(shape, 1)
    tile = ((c // 8) % GRID) * RING + (info[Q] + RING - c // 128) % RING
    hit = (rowid[...] == tile) & ((r // SLOTS) % 4 == c % 4)
    for half in range(2):
        pick = hit & ((c // 4) % 2 == half)
        out[:, half * 512 : half * 512 + 512] = nn(pick.astype(F32).astype(BF), table).astype(BF)


def sum_body(info, rowid, b, keep, came, across, z0, z1, z2, z3):
    rows = RING * GRID * 8
    shape = (rows, GRID * 4 * SLOTS)
    r, c = iota(shape, 0), iota(shape, 1)
    target = ((r // 8) % GRID) * RING + (info[Q] + RING - r // 128) % RING
    pick = (rowid[...] == target) & (r % 8 == (c // SLOTS) % 4)
    strips = nn(pick.astype(F32).astype(BF), b[...])
    grads = keep[...].astype(F32) + came[...].astype(F32)
    grads = (grads.reshape(256, D) + across[...].astype(F32)).astype(BF)
    shape = (rows, 256)
    r, c = iota(shape, 0), iota(shape, 1)
    source = ((r // 8) % GRID) * 16 + ((info[Q] + RING - r // 128) % RING) * 4 + r % 8 - 4
    pick = (r % 8 >= 4) & (c == source)
    total = (strips + nn(pick.astype(F32).astype(BF), grads)).astype(BF)
    for i, z in enumerate((z0, z1, z2, z3)):
        z[...] = total[i * 128 : i * 128 + 128]


def final_body(info, strip_rows, gk, gv, ret, r_in, gk_out, gv_out, w_out):
    shape = (GRID * 8, TILE)
    r, t = iota(shape, 0), iota(shape, 1)
    hit = strip_target(info, strip_rows, shape, 8) == t
    arrived = r_in[...]
    for part, (grad, out) in enumerate(((gk, gk_out), (gv, gv_out))):
        for f in range(2):
            pick = hit & (r % 8 == 2 * f + part)
            total = grad[f] + tn(pick.astype(F32).astype(BF), arrived)
            if f == 1:
                total = total + ret[part].astype(F32)
            out[f] = total.astype(BF)
    shape = (8, GRID * 8)
    pick = iota(shape, 0) + 4 == iota(shape, 1) % 8
    w_out[...] = nn(pick.astype(F32).astype(BF), arrived)[:4]


def on_device(
    queries, key_vectors, value_vectors, w_out, rig_tiles, rig_count, strip_rows, cotangent
):
    cam = lax.axis_index("cam")
    tm = lax.axis_index("tm")
    core, zlo = tm % 2, tm // 2
    ring = cam % RING
    steps = jnp.arange(8, dtype=jnp.int32)
    order = (((zlo ^ (1 - (steps >> 1) % 2)) * 2 + (core ^ (1 - (steps >> 2)))) * 2 + steps % 2)
    count = lax.dynamic_index_in_dim(rig_count, cam, 0, keepdims=False)
    zero = jnp.zeros((), jnp.int32)
    info = jnp.concatenate([jnp.stack([core, zlo, tm, ring, cam, count, zero, zero]), order])
    info = info.astype(jnp.int32)

    q = queries.reshape(2, TILE, D)
    k = key_vectors.reshape(2, TILE, D)
    v = value_vectors.reshape(2, TILE, D)
    cot = cotangent.reshape(2, TILE, D)

    plane = [[p * RING + z for p in range(GRID)] for z in range(RING)]

    def exchange(block):
        return lax.all_to_all(block, "cam", 0, 0, axis_index_groups=plane, tiled=True)

    def along_ring(block, shift):
        route = [
            (p * RING + z, p * RING + (z + shift) % RING)
            for p in range(GRID)
            for z in range(RING)
        ]
        return lax.ppermute(block, "cam", route)

    rigs = lax.dynamic_index_in_dim(rig_tiles.reshape(GRID, RING, 7), ring, 1, keepdims=False)
    counts = lax.dynamic_index_in_dim(rig_count.reshape(GRID, RING), ring, 1, keepdims=False)
    rigs = jnp.where(jnp.arange(7, dtype=jnp.int32) < counts[:, None], rigs, -1)
    rigs = jnp.pad(rigs, ((0, 0), (0, 1)), constant_values=-1)
    rowid = jnp.broadcast_to(rigs[:, None], (GRID, 4, SLOTS)).reshape(-1)

    pair = lambda i, *_: (0, 0, i)
    row = lambda i, *_: (i, 0)
    head = lambda i, *_: (i, 0, 0)
    head4 = lambda i, *_: (i, 0, 0, 0)
    blk = (2, TILE, TILE)

    mine, last = call(
        extract_body,
        (1,),
        [info, strip_rows, (k, None, None), (v, None, None)],
        [(like((GRID * 8, 512)), None, None), (like((2, TILE, D)), None, None)],
        16,
        1 << 27,
        2 << 20,
        scalars=2,
    )
    prev = lax.ppermute(last, "tm", [(i, i + 1) for i in range(3)])
    t0 = exchange(mine.reshape(GRID, 8, 512)).reshape(GRID * 8, 512)
    t1, t2, t3 = [along_ring(t0, s) for s in (1, 2, 3)]

    g, gt, m1, l1, o1 = call(
        local_body,
        (PAIRS,),
        [
            info,
            (q, blk, pair),
            (k, blk, pair),
            (v, blk, pair),
            (prev, blk, pair),
            (cot, None, None),
            (w_out, (TILE, D), row),
        ],
        [
            (like((2, TILE, D)), blk, pair),
            (like((D, 2 * TILE)), (TILE, 2 * TILE), row),
            (like((PAIRS, 2, 256), F32), (1, 2, 256), head),
            (like((PAIRS, 2, 256), F32), (1, 2, 256), head),
            (like((PAIRS, 2, TILE, TILE), F32), (1, 2, TILE, TILE), head4),
        ],
        24,
        3 << 30,
        8 << 20,
    )

    (sends,) = call(
        select_body,
        (1,),
        [info, (rowid.reshape(-1, 1), None, None)] + [(t, None, None) for t in (t0, t1, t2, t3)],
        [(like((GRID * 4 * SLOTS, D)), None, None)],
        24,
        1 << 29,
        2 << 20,
    )
    strips = exchange(sends.reshape(GRID, 4 * SLOTS, D)).reshape(GRID, 4, SLOTS, D)

    opair = lambda i, info: (0, 0, info[ORDER + i])
    orow = lambda i, info: (info[ORDER + i], 0)
    ohead = lambda i, info: (info[ORDER + i], 0, 0)
    ohead4 = lambda i, info: (info[ORDER + i], 0, 0, 0)
    sblk = (GRID, 4, SLOTS, TILE)
    spair = lambda i, info: (0, 0, 0, info[ORDER + i])
    stat = (like((PAIRS, 2, 256), F32), (1, 2, 256), ohead)
    att, back, m, rl, delta, dq, w_send, w_keep = call(
        strip_body,
        (PAIRS,),
        [
            info,
            (q, blk, opair),
            (g, blk, opair),
            (gt, (TILE, 2 * TILE), orow),
            (strips, sblk, spair),
            (m1, (1, 2, 256), ohead),
            (l1, (1, 2, 256), ohead),
            (o1, (1, 2, TILE, TILE), ohead4),
            (cot, None, None),
        ],
        [
            (like((2, TILE, D)), blk, opair),
            (like((GRID, 4, SLOTS, D)), sblk, spair),
            stat,
            stat,
            stat,
            (like((PAIRS, 2, TILE, TILE), F32), (1, 2, TILE, TILE), ohead4),
            (like((4, TILE, D)), (1, TILE, D), lambda i, info: (jnp.minimum(i, 3), 0, 0)),
            (like((4, TILE, D)), (1, TILE, D), lambda i, info: (jnp.maximum(i - 4, 0), 0, 0)),
        ],
        24,
        2 << 30,
        10 << 20,
    )
    came = lax.ppermute(w_send, "tm", [(i, i ^ 1) for i in range(4)])
    half = (w_keep[:2].astype(F32) + came[:2].astype(F32)).astype(BF).reshape(2 * TILE, D)
    across = lax.ppermute(half, "tm", [(i, i ^ 2) for i in range(4)])
    b = exchange(back.reshape(GRID, 4 * SLOTS, D)).reshape(GRID * 4 * SLOTS, D)

    upper = ((2, TILE, D), lambda *_: (1, 0, 0))
    zs = call(
        sum_body,
        (1,),
        [
            info,
            (rowid.reshape(1, -1), None, None),
            (b, None, None),
            (w_keep,) + upper,
            (came,) + upper,
            (across, None, None),
        ],
        [(like((GRID * 8, D)), None, None)] * 4,
        32,
        1 << 30,
        4 << 20,
    )
    pieces = [zs[0]] + [along_ring(zs[s], -s) for s in (1, 2, 3)]

    gq, gk, gv, ret, mixed = call(
        back_body,
        (PAIRS,),
        [
            info,
            (q, blk, pair),
            (k, blk, pair),
            (v, blk, pair),
            (prev, blk, pair),
            (g, blk, pair),
            (m, (1, 2, 256), head),
            (rl, (1, 2, 256), head),
            (delta, (1, 2, 256), head),
            (dq, (1, 2, TILE, TILE), head4),
            (att, None, None),
            (w_out, (D, TILE), lambda i, *_: (0, i)),
        ],
        [
            (like((2, TILE, D)), blk, pair),
            (like((2, TILE, D), F32), blk, pair),
            (like((2, TILE, D), F32), blk, pair),
            (like((2, TILE, D)), blk, pair),
            (like((2, TILE, D)), blk, pair),
        ],
        24,
        4 << 30,
        12 << 20,
    )
    returned = lax.ppermute(ret, "tm", [(i + 1, i) for i in range(3)])
    summed = functools.reduce(jnp.add, [z.astype(F32) for z in pieces]).astype(BF)
    arrived = exchange(summed.reshape(GRID, 8, D)).reshape(GRID * 8, D)

    quarter = (2, TILE, 256)
    grad_k, grad_v, grad_w = call(
        final_body,
        (4,),
        [
            info,
            strip_rows,
            (gk, quarter, pair),
            (gv, quarter, pair),
            (returned, quarter, pair),
            (arrived, (GRID * 8, 256), lambda i, *_: (0, i)),
        ],
        [
            (like((2, TILE, D)), quarter, pair),
            (like((2, TILE, D)), quarter, pair),
            (like((4, D), F32), (4, 256), lambda i, *_: (0, i)),
        ],
        24,
        1 << 27,
        4 << 20,
        scalars=2,
    )
    whole = (2, 1, TILE, D)
    return (
        mixed.reshape(whole),
        gq.reshape(whole),
        grad_k.reshape(whole),
        grad_v.reshape(whole),
        grad_w,
    )


def solution(mesh):
    block = P("tm", "cam", None, None)
    return jax.shard_map(
        on_device,
        mesh=mesh,
        in_specs=(block, block, block, P(), P(), P(), P(), block),
        out_specs=(block, block, block, block, P(("tm", "cam"), None)),
        check_vma=False,
    )
```

```python
import functools

import jax
import jax.numpy as jnp
from jax import lax
from jax.experimental import pallas as pl
from jax.experimental.pallas import tpu as pltpu
from jax.sharding import PartitionSpec as P

TILE = 128
D = 1024
PAIRS = 8
RING = 4
GRID = 16
SLOTS = 8
NEG = -1e30
BF = jnp.bfloat16
F32 = jnp.float32
MIB = 1 << 20

TM, CAM = range(2)
BLOCKS = 4
WIDE = 2 * TILE
AFTER = "after"


def nt(a, b):
    return lax.dot_general(a, b, (((1,), (1,)), ((), ())), preferred_element_type=F32)


def tn(a, b):
    return lax.dot_general(a, b, (((0,), (0,)), ((), ())), preferred_element_type=F32)


def nn(a, b):
    return jnp.dot(a, b, preferred_element_type=F32)


def iota(shape, dim):
    return lax.broadcasted_iota(jnp.int32, shape, dim)


def call(body, grid, inputs, outputs, limit_mib, flops, nbytes, scalars=1):
    def spec(entry):
        shape, block, index = entry
        if block == AFTER:
            return pl.BlockSpec(memory_space=pl.ANY)
        if block is None:
            zeros = (0,) * len(shape.shape)
            return pl.BlockSpec(shape.shape, lambda *_: zeros)
        return pl.BlockSpec(block, index)

    return pl.pallas_call(
        body,
        grid_spec=pltpu.PrefetchScalarGridSpec(
            num_scalar_prefetch=scalars,
            grid=grid,
            in_specs=[spec(e) for e in inputs[scalars:]],
            out_specs=[spec(e) for e in outputs],
        ),
        out_shape=[e[0] for e in outputs],
        compiler_params=pltpu.CompilerParams(vmem_limit_bytes=limit_mib * MIB),
        cost_estimate=pl.CostEstimate(flops=flops, bytes_accessed=nbytes, transcendentals=0),
    )(*[e[0] if isinstance(e, tuple) else e for e in inputs])


def like(shape, dtype=BF):
    return jax.ShapeDtypeStruct(shape, dtype)


def strip_target(info, strip_rows, shape, group):
    s = iota(shape, 0) // group
    target = jnp.zeros(shape, jnp.int32)
    for i in range(GRID):
        target = jnp.where(s == i, strip_rows[i, info[CAM]], target)
    return target


def ring_place(info, back):
    return (info[CAM] + RING - back) % RING


def extract_body(info, strip_rows, k, v, out, last):
    shape = (GRID * 8, 2 * TILE)
    r, c = iota(shape, 0), iota(shape, 1)
    hit = (strip_target(info, strip_rows, shape, 8) == c % TILE) & ((r // 2) % 2 == c // TILE)
    total = jnp.zeros((GRID * 8, D // 2), F32)
    for part, ref in enumerate((k, v)):
        whole = ref[...].reshape(2 * TILE, D)
        for half in range(2):
            pick = hit & (r % 2 == part) & ((r // 4) % 2 == half)
            total += nn(pick.astype(F32).astype(BF), whole[:, half * 512 : half * 512 + 512])
        last[part] = ref[1]
    out[...] = total.astype(BF)


def stacked(block):
    first = iota(block.shape, 1) < 64
    zero = jnp.zeros_like(block)
    return jnp.concatenate([jnp.where(first, block, zero), jnp.where(first, zero, block)], 0)


def own_half(wide):
    return jnp.concatenate([wide[:64, :TILE], wide[64:, TILE:]], 0)


def spread(row):
    return jnp.concatenate(
        [jnp.broadcast_to(row[:, :TILE], (64, TILE)), jnp.broadcast_to(row[:, TILE:], (64, TILE))],
        0,
    )


def units():
    return [(n, slice(n * TILE, n * TILE + TILE), f) for n in range(2) for f in range(2)]


def grad_body(cot, w, g_out, gt_out):
    cots = cot[...].reshape(2 * TILE, D)
    g_out[...] = nt(cots, w[...]).astype(BF).reshape(2, TILE, WIDE)
    gt_out[...] = nt(w[...], cots).astype(BF)


def copy_body(block, _, out):
    out[...] = block[...]


def local_body(info, q, k, v, prev, _, m_out, l_out, o_out):
    for n, at, f in units():
        qs = stacked(q[f, :, at] * jnp.asarray(0.125, BF))
        before_k, before_v = (prev[0, :, at], prev[1, :, at]) if f == 0 else (k[0, :, at], v[0, :, at])
        s1 = nt(k[f, :, at], qs)
        s2 = nt(before_k, qs)
        if f == 0:
            s2 = jnp.where(info[TM] > 0, s2, NEG)
        m = jnp.maximum(jnp.max(s1, 0, keepdims=True), jnp.max(s2, 0, keepdims=True))
        p1 = jnp.exp(s1 - m)
        p2 = jnp.exp(s2 - m)
        m_out[n, f] = m[0]
        l_out[n, f] = jnp.sum(p1, 0) + jnp.sum(p2, 0)
        o_out[n, f] = own_half(tn(v[f, :, at], p1.astype(BF)) + tn(before_v, p2.astype(BF)))


def strip_body(
    info, rig_count, q, g, gt, strips, m1, l1, o1, _,
    back, m_out, rl_out, delta_out, dq_out, *ot_out,
):
    seen = iota((TILE, WIDE), 0) % SLOTS < rig_count[info[CAM]]
    ots = {}
    for n, at, f in units():
        qs = stacked(q[f, :, at] * jnp.asarray(0.125, BF))
        gs = stacked(g[f, :, at])
        ks = strips[:, 2 * f, :, at].astype(F32).reshape(TILE, TILE).astype(BF)
        vs = strips[:, 2 * f + 1, :, at].astype(F32).reshape(TILE, TILE).astype(BF)
        s = jnp.where(seen, nt(ks, qs), NEG)
        m_old = m1[n, f : f + 1]
        m = jnp.maximum(m_old, jnp.max(s, 0, keepdims=True))
        p = jnp.exp(s - m)
        shrink = jnp.exp(m_old - m)
        rl = 1.0 / (l1[n, f : f + 1] * shrink + jnp.sum(p, 0, keepdims=True))
        p = p * rl
        pb = p.astype(BF)
        ot = (o1[n, f] * spread(shrink * rl) + own_half(tn(vs, pb))).astype(BF)
        prod = gt[at, f * TILE : f * TILE + TILE].astype(F32) * ot.astype(F32)
        delta = jnp.concatenate(
            [jnp.sum(prod[:64], 0, keepdims=True), jnp.sum(prod[64:], 0, keepdims=True)], 1
        )
        ds = (p * (nt(vs, gs) - delta)).astype(BF)
        back[:, 2 * f, :, at] = nn(ds, qs).reshape(GRID, SLOTS, TILE).astype(BF)
        back[:, 2 * f + 1, :, at] = nn(pb, gs).reshape(GRID, SLOTS, TILE).astype(BF)
        dq_out[n, f] = own_half(tn(ks, ds))
        m_out[n, f] = m[0]
        rl_out[n, f] = rl[0]
        delta_out[n, f] = delta[0]
        ots[n, f] = ot
    whole = jnp.concatenate([jnp.concatenate([ots[n, 0], ots[n, 1]], 1) for n in range(2)], 0)
    for i, out in enumerate(ot_out):

        @pl.when(pl.program_id(0) == i)
        def _():
            out[...] = whole


def weight_body(info, c0, c1, c2, c3, ot0, ot1, ot2, ot3, _, e0, e1, e2, e3):
    total = jnp.zeros((WIDE, D), F32)
    for ot, c in ((ot0, c0), (ot1, c1), (ot2, c2), (ot3, c3)):
        total += nn(ot[...], c[...].reshape(WIDE, D))
    total = total.astype(BF)
    shape = (RING * GRID * 8, WIDE)
    r, c = iota(shape, 0), iota(shape, 1)
    hit = c == ((r // 8) % GRID) * 16 + ring_place(info, r // 128) * 4 + r % 4
    out = jnp.zeros((RING * GRID * 8, D // 2), F32)
    for half in range(2):
        pick = hit & ((r // 4) % 2 == half)
        out += nn(pick.astype(F32).astype(BF), total[:, half * 512 : half * 512 + 512])
    out = out.astype(BF)
    for i, e in enumerate((e0, e1, e2, e3)):
        e[...] = out[i * 128 : i * 128 + 128]


def mixed_body(info, ot0, ot1, ot2, ot3, w, _, out):
    total = jnp.zeros((WIDE, 512), F32)
    for i, ot in enumerate((ot0, ot1, ot2, ot3)):
        total += tn(ot[...], w[pl.ds((info[TM] ^ i) * WIDE, WIDE)])
    out[...] = total.astype(BF).reshape(2, TILE, 512)


def block_back(kb, vb, qs, gs, m, rl, delta, hidden=None):
    s = nt(kb, qs)
    if hidden is not None:
        s = jnp.where(hidden, NEG, s)
    p = jnp.exp(s - m) * rl
    ds = (p * (nt(vb, gs) - delta)).astype(BF)
    return nn(ds, qs), nn(p.astype(BF), gs), own_half(tn(kb, ds))


def before_body(info, q, prev, g, m, rl, delta, dq, ret_out, dq_out):
    for n in range(4):
        at = slice(n * TILE, n * TILE + TILE)
        qs = stacked(q[0, :, at] * jnp.asarray(0.125, BF))
        gs = stacked(g[0, :, at])
        dk, dv, part = block_back(
            prev[0, :, at], prev[1, :, at], qs, gs, m[n, :1], rl[n, :1], delta[n, :1],
            info[TM] == 0,
        )
        ret_out[0, :, at] = dk.astype(BF)
        ret_out[1, :, at] = dv.astype(BF)
        dq_out[n] = dq[n, 0] + part


def back_body(
    info, q, k, v, g, m, rl, delta, dq0, dq, _, __, ___, ____, gq_out, gk_out, gv_out
):
    for n in range(2):
        at = slice(n * TILE, n * TILE + TILE)
        for f in range(2):
            qs = stacked(q[f, :, at] * jnp.asarray(0.125, BF))
            gs = stacked(g[f, :, at])
            stats = m[n, f : f + 1], rl[n, f : f + 1], delta[n, f : f + 1]
            dk, dv, part = block_back(k[f, :, at], v[f, :, at], qs, gs, *stats)
            if f == 0:
                total, dk0, dv0 = dq0[n] + part, dk, dv
            else:
                gk_out[1, :, at] = dk
                gv_out[1, :, at] = dv
                dk, dv, before = block_back(k[0, :, at], v[0, :, at], qs, gs, *stats)
                gk_out[0, :, at] = dk0 + dk
                gv_out[0, :, at] = dv0 + dv
                total = dq[n, 0] + part + before
            gq_out[f, :, at] = (total * 0.125).T.astype(BF)


def select_body(info, rowid, t0, t1, t2, t3, _, out):
    table = jnp.concatenate([t0[...], t1[...], t2[...], t3[...]], 0)
    shape = (GRID * 4 * SLOTS, RING * GRID * 8)
    r, c = iota(shape, 0), iota(shape, 1)
    tile = ((c // 8) % GRID) * RING + ring_place(info, c // 128)
    hit = (rowid[...] == tile) & ((r // SLOTS) % 4 == c % 4)
    for half in range(2):
        pick = hit & ((c // 4) % 2 == half)
        out[:, half * 512 : half * 512 + 512] = nn(pick.astype(F32).astype(BF), table).astype(BF)


def sum_body(info, rowid, b, z0, z1, z2, z3):
    rows = RING * GRID * 8
    shape = (rows, GRID * 4 * SLOTS)
    r, c = iota(shape, 0), iota(shape, 1)
    target = ((r // 8) % GRID) * RING + ring_place(info, r // 128)
    hit = (rowid[...] == target) & (r % 4 == (c // SLOTS) % 4)
    total = jnp.zeros((rows, D // 2), F32)
    for half in range(2):
        pick = hit & ((r // 4) % 2 == half)
        total += nn(pick.astype(F32).astype(BF), b[:, half * 512 : half * 512 + 512])
    total = total.astype(BF)
    for i, z in enumerate((z0, z1, z2, z3)):
        z[...] = total[i * 128 : i * 128 + 128]


def merge_body(z0, z1, z2, z3, e0, e1, e2, e3, _, out):
    def total(parts):
        return functools.reduce(jnp.add, [part[...].astype(F32) for part in parts])

    out[...] = jnp.concatenate([total((z0, z1, z2, z3)), total((e0, e1, e2, e3))], 1).astype(BF)


def final_body(info, strip_rows, gk, gv, ret, r_in, gk_out, gv_out, w_out):
    half = pl.program_id(0) // 2
    shape = (GRID * 16, TILE)
    r, t = iota(shape, 0), iota(shape, 1)
    hit = strip_target(info, strip_rows, shape, 16) == t
    arrived = r_in[...]
    for part, (grad, out) in enumerate(((gk, gk_out), (gv, gv_out))):
        for f in range(2):
            pick = hit & (r % 16 == half * 4 + 2 * f + part)
            total = grad[f] + tn(pick.astype(F32).astype(BF), arrived)
            if f == 1:
                total = total + ret[part].astype(F32)
            out[f] = total.astype(BF)
    shape = (8, GRID * 16)
    pick = iota(shape, 1) % 16 == 8 + half * 4 + iota(shape, 0)
    w_out[...] = nn(pick.astype(F32).astype(BF), arrived)[:4]


def on_device(
    queries, key_vectors, value_vectors, w_out, rig_tiles, rig_count, strip_rows, cotangent
):
    cam = lax.axis_index("cam")
    tm = lax.axis_index("tm")
    ring = cam % RING
    info = jnp.stack([tm, cam]).astype(jnp.int32)
    strip_rows = strip_rows.T

    q = queries.reshape(2, TILE, D)
    k = key_vectors.reshape(2, TILE, D)
    v = value_vectors.reshape(2, TILE, D)
    cot = cotangent.reshape(2, TILE, D)

    plane = [[p * RING + z for p in range(GRID)] for z in range(RING)]

    def exchange(block):
        return lax.all_to_all(block, "cam", 0, 0, axis_index_groups=plane, tiled=True)

    def along_ring(block, shift):
        route = [
            (p * RING + z, p * RING + (z + shift) % RING)
            for p in range(GRID)
            for z in range(RING)
        ]
        return lax.ppermute(block, "cam", route)

    rigs = lax.dynamic_index_in_dim(rig_tiles.reshape(GRID, RING, 7), ring, 1, keepdims=False)
    counts = lax.dynamic_index_in_dim(rig_count.reshape(GRID, RING), ring, 1, keepdims=False)
    rigs = jnp.where(jnp.arange(7, dtype=jnp.int32) < counts[:, None], rigs, -1)
    rigs = jnp.pad(rigs, ((0, 0), (0, 1)), constant_values=-1)
    rowid = jnp.broadcast_to(rigs[:, None], (GRID, 4, SLOTS)).reshape(-1)

    pair = lambda i, *_: (0, 0, i)
    row = lambda i, *_: (i, 0)
    head = lambda i, *_: (i, 0, 0)
    head4 = lambda i, *_: (i, 0, 0, 0)
    blk = (2, TILE, WIDE)
    stats, sblk = like((PAIRS, 2, WIDE), F32), (2, 2, WIDE)
    heads, hblk = like((PAIRS, 2, TILE, TILE), F32), (2, 2, TILE, TILE)
    act = like((2, TILE, D))

    mine, last = call(
        extract_body,
        (1,),
        [info, strip_rows, (k, None, None), (v, None, None)],
        [(like((GRID * 8, 512)), None, None), (act, None, None)],
        60,
        1 << 27,
        2 << 20,
        scalars=2,
    )
    prev = lax.ppermute(last, "tm", [(i, i + 1) for i in range(3)])
    t0 = exchange(mine.reshape(GRID, 8, 512)).reshape(GRID * 8, 512)
    t1, t2, t3 = [along_ring(t0, s) for s in (1, 2, 3)]

    g, gt = call(
        grad_body,
        (BLOCKS,),
        [(cot, None, None), (w_out, (WIDE, D), row)],
        [(act, blk, pair), (like((D, WIDE)), (WIDE, WIDE), row)],
        60,
        1 << 30,
        4 << 20,
        scalars=0,
    )
    m1, l1, o1 = call(
        local_body,
        (BLOCKS,),
        [
            info,
            (q, blk, pair),
            (k, blk, pair),
            (v, blk, pair),
            (prev, blk, pair),
            (t0, AFTER, None),
        ],
        [
            (stats, sblk, head),
            (stats, sblk, head),
            (heads, hblk, head4),
        ],
        60,
        1 << 30,
        4 << 20,
    )

    (sends,) = call(
        select_body,
        (1,),
        [info, (rowid.reshape(-1, 1), None, None)]
        + [(t, None, None) for t in (t0, t1, t2, t3)]
        + [(m1, AFTER, None)],
        [(like((GRID * 4 * SLOTS, D)), None, None)],
        60,
        1 << 29,
        2 << 20,
    )
    (cot0,) = call(
        copy_body,
        (1,),
        [(cot, None, None), (sends, AFTER, None)],
        [(act, None, None)],
        60,
        1 << 20,
        1 << 20,
        scalars=0,
    )
    cot1 = lax.ppermute(cot0, "tm", [(t, t ^ 1) for t in range(4)])
    cot2 = lax.ppermute(cot0, "tm", [(t, t ^ 2) for t in range(4)])
    cot3 = lax.ppermute(cot2, "tm", [(t, t ^ 1) for t in range(4)])
    strips = exchange(sends.reshape(GRID, 4 * SLOTS, D)).reshape(GRID, 4, SLOTS, D)

    def block_of(i, info):
        return info[TM] ^ i

    opair = lambda i, info, _: (0, 0, block_of(i, info))
    orow = lambda i, info, _: (block_of(i, info), 0)
    ohead = lambda i, info, _: (block_of(i, info), 0, 0)
    ohead4 = lambda i, info, _: (block_of(i, info), 0, 0, 0)
    gblk = (GRID, 4, SLOTS, WIDE)
    gpair = lambda i, info, _: (0, 0, 0, block_of(i, info))
    back, m, rl, delta, dq, *ots = call(
        strip_body,
        (BLOCKS,),
        [
            info,
            rig_count,
            (q, blk, opair),
            (g, blk, opair),
            (gt, (WIDE, WIDE), orow),
            (strips, gblk, gpair),
            (m1, sblk, ohead),
            (l1, sblk, ohead),
            (o1, hblk, ohead4),
            (cot2, AFTER, None),
        ],
        [
            (like((GRID, 4, SLOTS, D)), gblk, gpair),
            (stats, sblk, ohead),
            (stats, sblk, ohead),
            (stats, sblk, ohead),
            (heads, hblk, ohead4),
        ]
        + [(like((WIDE, WIDE)), None, None)] * 4,
        60,
        2 << 30,
        10 << 20,
        scalars=2,
    )
    own_ots = ots
    ots = [ots[0]] + [
        lax.ppermute(ots[i], "tm", [(t, t ^ i) for t in range(4)]) for i in (1, 2, 3)
    ]
    front, wide = (1, TILE, 4 * TILE), (2, TILE, 4 * TILE)
    wstat = (4, 2, WIDE)
    ret, dq0 = call(
        before_body,
        (2,),
        [
            info,
            (q, front, pair),
            (prev, wide, pair),
            (g, front, pair),
            (m, wstat, head),
            (rl, wstat, head),
            (delta, wstat, head),
            (dq, (4, 1, TILE, TILE), head4),
        ],
        [(act, wide, pair), (like((PAIRS, TILE, TILE), F32), (4, TILE, TILE), head)],
        60,
        1 << 29,
        4 << 20,
    )
    returned = lax.ppermute(ret, "tm", [(i + 1, i) for i in range(3)])
    b = exchange(back.reshape(GRID, 4 * SLOTS, D)).reshape(GRID * 4 * SLOTS, D)

    piece = (like((GRID * 8, 512)), None, None)
    es = call(
        weight_body,
        (1,),
        [info] + [(o, None, None) for o in (cot, cot1, cot2, cot3, *ots)] + [(ret, AFTER, None)],
        [piece] * 4,
        60,
        1 << 30,
        6 << 20,
    )
    es = [es[0]] + [along_ring(es[s], -s) for s in (1, 2, 3)]

    zs = call(
        sum_body,
        (1,),
        [info, (rowid.reshape(1, -1), None, None), (b, None, None)],
        [piece] * 4,
        10,
        1 << 29,
        2 << 20,
    )
    pieces = [zs[0]] + [along_ring(zs[s], -s) for s in (1, 2, 3)]

    gq, gk, gv = call(
        back_body,
        (BLOCKS,),
        [
            info,
            (q, blk, pair),
            (k, blk, pair),
            (v, blk, pair),
            (g, blk, pair),
            (m, sblk, head),
            (rl, sblk, head),
            (delta, sblk, head),
            (dq0, (2, TILE, TILE), head),
            (dq, (2, 1, TILE, TILE), lambda i, *_: (i, 1, 0, 0)),
            (pieces[1], AFTER, None),
        ]
        + [(e, AFTER, None) for e in es[1:]],
        [
            (act, blk, pair),
            (like((2, TILE, D), F32), blk, pair),
            (like((2, TILE, D), F32), blk, pair),
        ],
        60,
        2 << 30,
        8 << 20,
    )

    (summed,) = call(
        merge_body,
        (1,),
        [(x.reshape(GRID, 8, 512), None, None) for x in pieces + es] + [(gq, AFTER, None)],
        [(like((GRID, 16, 512)), None, None)],
        60,
        1 << 20,
        1 << 20,
        scalars=0,
    )
    arrived = exchange(summed).reshape(GRID * 16, 512)
    (mixed,) = call(
        mixed_body,
        (2,),
        [info]
        + [(o, None, None) for o in own_ots]
        + [(w_out, (D, 512), lambda i, *_: (0, i)), (summed, AFTER, None)],
        [(act, (2, TILE, 512), pair)],
        60,
        1 << 29,
        4 << 20,
    )

    quarter = (2, TILE, 256)
    grad_k, grad_v, grad_w = call(
        final_body,
        (4,),
        [
            info,
            strip_rows,
            (gk, quarter, pair),
            (gv, quarter, pair),
            (returned, quarter, pair),
            (arrived, (GRID * 16, 256), lambda i, *_: (0, i % 2)),
        ],
        [
            (act, quarter, pair),
            (act, quarter, pair),
            (like((4, D), F32), (4, 256), lambda i, *_: (0, i)),
        ],
        60,
        1 << 27,
        4 << 20,
        scalars=2,
    )
    whole = (2, 1, TILE, D)
    return (
        mixed.reshape(whole),
        gq.reshape(whole),
        grad_k.reshape(whole),
        grad_v.reshape(whole),
        grad_w,
    )


def solution(mesh):
    block = P("tm", "cam", None, None)
    return jax.shard_map(
        on_device,
        mesh=mesh,
        in_specs=(block, block, block, P(), P(), P(), P(), block),
        out_specs=(block, block, block, block, P(("tm", "cam"), None)),
        check_vma=False,
    )
```

```python
import functools

import jax
import jax.numpy as jnp
from jax import lax
from jax.experimental import pallas as pl
from jax.experimental.pallas import tpu as pltpu
from jax.sharding import PartitionSpec as P

TILE = 128
D = 1024
PAIRS = 8
RING = 4
GRID = 16
SLOTS = 8
NEG = -1e30
BF = jnp.bfloat16
F32 = jnp.float32
MIB = 1 << 20

TM, CAM = range(2)
BLOCKS = 4
WIDE = 2 * TILE
AFTER, NEAR, FAR = "after", "near", "far"


def nt(a, b):
    return lax.dot_general(a, b, (((1,), (1,)), ((), ())), preferred_element_type=F32)


def tn(a, b):
    return lax.dot_general(a, b, (((0,), (0,)), ((), ())), preferred_element_type=F32)


def nn(a, b):
    return jnp.dot(a, b, preferred_element_type=F32)


def iota(shape, dim):
    return lax.broadcasted_iota(jnp.int32, shape, dim)


def call(body, grid, inputs, outputs, limit_mib, flops, nbytes, scalars=1):
    def space(entry):
        return pltpu.VMEM if entry[-1] == NEAR else pltpu.HBM

    def place(entry):
        if not isinstance(entry, tuple):
            return entry
        if entry[1:] == (AFTER, None):
            return entry[0]
        return pltpu.with_memory_space_constraint(entry[0], space(entry))

    def spec(entry):
        shape, block, index = entry[:3]
        if block == AFTER:
            return pl.BlockSpec(memory_space=pl.ANY)
        if block is None:
            zeros = (0,) * len(shape.shape)
            return pl.BlockSpec(shape.shape, lambda *_: zeros)
        return pl.BlockSpec(block, index)

    return pl.pallas_call(
        body,
        grid_spec=pltpu.PrefetchScalarGridSpec(
            num_scalar_prefetch=scalars,
            grid=grid,
            in_specs=[spec(e) for e in inputs[scalars:]],
            out_specs=[spec(e) for e in outputs],
        ),
        out_shape=[space(e)(e[0].shape, e[0].dtype) for e in outputs],
        compiler_params=pltpu.CompilerParams(vmem_limit_bytes=limit_mib * MIB),
        cost_estimate=pl.CostEstimate(flops=flops, bytes_accessed=nbytes, transcendentals=0),
    )(*[place(e) for e in inputs])


def like(shape, dtype=BF):
    return jax.ShapeDtypeStruct(shape, dtype)


def strip_target(info, strip_rows, shape, group):
    s = iota(shape, 0) // group
    target = jnp.zeros(shape, jnp.int32)
    for i in range(GRID):
        target = jnp.where(s == i, strip_rows[i, info[CAM]], target)
    return target


def ring_place(info, back):
    return (info[CAM] + RING - back) % RING


def extract_body(info, strip_rows, k, v, out, last):
    shape = (GRID * 8, 2 * TILE)
    r, c = iota(shape, 0), iota(shape, 1)
    hit = (strip_target(info, strip_rows, shape, 8) == c % TILE) & ((r // 2) % 2 == c // TILE)
    total = jnp.zeros((GRID * 8, D // 2), F32)
    for part, ref in enumerate((k, v)):
        whole = ref[...].reshape(2 * TILE, D)
        for half in range(2):
            pick = hit & (r % 2 == part) & ((r // 4) % 2 == half)
            total += nn(pick.astype(F32).astype(BF), whole[:, half * 512 : half * 512 + 512])
        last[part] = ref[1]
    out[...] = total.astype(BF)


def stacked(block):
    first = iota(block.shape, 1) < 64
    zero = jnp.zeros_like(block)
    return jnp.concatenate([jnp.where(first, block, zero), jnp.where(first, zero, block)], 0)


def own_half(wide):
    return jnp.concatenate([wide[:64, :TILE], wide[64:, TILE:]], 0)


def spread(row):
    return jnp.concatenate(
        [jnp.broadcast_to(row[:, :TILE], (64, TILE)), jnp.broadcast_to(row[:, TILE:], (64, TILE))],
        0,
    )


def units():
    return [(n, slice(n * TILE, n * TILE + TILE), f) for n in range(2) for f in range(2)]


def grad_body(cot, w, g_out, gt_out):
    cots = cot[...].reshape(2 * TILE, D)
    g_out[...] = nt(cots, w[...]).astype(BF).reshape(2, TILE, WIDE)
    gt_out[...] = nt(w[...], cots).astype(BF)


def local_body(info, q, k, v, prev, cot, _, m_out, l_out, o_out, cot_out):
    cot_out[...] = cot[...]
    for n, at, f in units():
        qs = stacked(q[f, :, at] * jnp.asarray(0.125, BF))
        before_k, before_v = (prev[0, :, at], prev[1, :, at]) if f == 0 else (k[0, :, at], v[0, :, at])
        s1 = nt(k[f, :, at], qs)
        s2 = nt(before_k, qs)
        if f == 0:
            s2 = jnp.where(info[TM] > 0, s2, NEG)
        m = jnp.maximum(jnp.max(s1, 0, keepdims=True), jnp.max(s2, 0, keepdims=True))
        p1 = jnp.exp(s1 - m)
        p2 = jnp.exp(s2 - m)
        m_out[n, f] = m[0]
        l_out[n, f] = jnp.sum(p1, 0) + jnp.sum(p2, 0)
        o_out[n, f] = own_half(tn(v[f, :, at], p1.astype(BF)) + tn(before_v, p2.astype(BF)))


def strip_body(
    info, rig_count, q, g, gt, strips, m1, l1, o1, _,
    back, m_out, rl_out, delta_out, dq_out, *ot_out,
):
    seen = iota((TILE, WIDE), 0) % SLOTS < rig_count[info[CAM]]
    ots = {}
    for n, at, f in units():
        qs = stacked(q[f, :, at] * jnp.asarray(0.125, BF))
        gs = stacked(g[f, :, at])
        ks = strips[:, 2 * f, :, at].astype(F32).reshape(TILE, TILE).astype(BF)
        vs = strips[:, 2 * f + 1, :, at].astype(F32).reshape(TILE, TILE).astype(BF)
        s = jnp.where(seen, nt(ks, qs), NEG)
        m_old = m1[n, f : f + 1]
        m = jnp.maximum(m_old, jnp.max(s, 0, keepdims=True))
        p = jnp.exp(s - m)
        shrink = jnp.exp(m_old - m)
        rl = 1.0 / (l1[n, f : f + 1] * shrink + jnp.sum(p, 0, keepdims=True))
        p = p * rl
        pb = p.astype(BF)
        ot = (o1[n, f] * spread(shrink * rl) + own_half(tn(vs, pb))).astype(BF)
        prod = gt[at, f * TILE : f * TILE + TILE].astype(F32) * ot.astype(F32)
        delta = jnp.concatenate(
            [jnp.sum(prod[:64], 0, keepdims=True), jnp.sum(prod[64:], 0, keepdims=True)], 1
        )
        ds = (p * (nt(vs, gs) - delta)).astype(BF)
        back[:, 2 * f, :, at] = nn(ds, qs).reshape(GRID, SLOTS, TILE).astype(BF)
        back[:, 2 * f + 1, :, at] = nn(pb, gs).reshape(GRID, SLOTS, TILE).astype(BF)
        dq_out[n, f] = own_half(tn(ks, ds))
        m_out[n, f] = m[0]
        rl_out[n, f] = rl[0]
        delta_out[n, f] = delta[0]
        ots[n, f] = ot
    whole = jnp.concatenate([jnp.concatenate([ots[n, 0], ots[n, 1]], 1) for n in range(2)], 0)
    for i, out in enumerate(ot_out):

        @pl.when(pl.program_id(0) == i)
        def _():
            out[...] = whole


def weight_body(info, c0, c1, c2, c3, ot0, ot1, ot2, ot3, e0, e1, e2, e3):
    total = jnp.zeros((WIDE, D), F32)
    for ot, c in ((ot0, c0), (ot1, c1), (ot2, c2), (ot3, c3)):
        total += nn(ot[...], c[...].reshape(WIDE, D))
    total = total.astype(BF)
    shape = (RING * GRID * 8, WIDE)
    r, c = iota(shape, 0), iota(shape, 1)
    hit = c == ((r // 8) % GRID) * 16 + ring_place(info, r // 128) * 4 + r % 4
    out = jnp.zeros((RING * GRID * 8, D // 2), F32)
    for half in range(2):
        pick = hit & ((r // 4) % 2 == half)
        out += nn(pick.astype(F32).astype(BF), total[:, half * 512 : half * 512 + 512])
    out = out.astype(BF)
    for i, e in enumerate((e0, e1, e2, e3)):
        e[...] = out[i * 128 : i * 128 + 128]


def mixed_body(info, ot0, ot1, ot2, ot3, w, _, out):
    total = jnp.zeros((WIDE, 512), F32)
    for i, ot in enumerate((ot0, ot1, ot2, ot3)):
        total += tn(ot[...], w[pl.ds((info[TM] ^ i) * WIDE, WIDE)])
    out[...] = total.astype(BF).reshape(2, TILE, 512)


def block_back(kb, vb, qs, gs, m, rl, delta, hidden=None):
    s = nt(kb, qs)
    if hidden is not None:
        s = jnp.where(hidden, NEG, s)
    p = jnp.exp(s - m) * rl
    ds = (p * (nt(vb, gs) - delta)).astype(BF)
    return nn(ds, qs), nn(p.astype(BF), gs), own_half(tn(kb, ds))


def back_body(
    info, q, k, v, prev, g, m, rl, delta, dq, _, gq_out, gk_out, gv_out, ret_out
):
    hidden = (iota((2 * TILE, WIDE), 0) >= TILE) & (info[TM] == 0)
    for n in range(2):
        at = slice(n * TILE, n * TILE + TILE)
        for f in range(2):
            qs = stacked(q[f, :, at] * jnp.asarray(0.125, BF))
            gs = stacked(g[f, :, at])
            before_k, before_v = (prev[0], prev[1]) if f == 0 else (k[0], v[0])
            keys = jnp.concatenate([k[f, :, at], before_k[:, at]], 0)
            values = jnp.concatenate([v[f, :, at], before_v[:, at]], 0)
            dk, dv, part = block_back(
                keys, values, qs, gs, m[n, f : f + 1], rl[n, f : f + 1], delta[n, f : f + 1],
                hidden if f == 0 else None,
            )
            if f == 0:
                dk0, dv0 = dk[:TILE], dv[:TILE]
                ret_out[0, :, at] = dk[TILE:].astype(BF)
                ret_out[1, :, at] = dv[TILE:].astype(BF)
            else:
                gk_out[1, :, at] = dk[:TILE]
                gv_out[1, :, at] = dv[:TILE]
                gk_out[0, :, at] = dk0 + dk[TILE:]
                gv_out[0, :, at] = dv0 + dv[TILE:]
            gq_out[f, :, at] = ((dq[n, f] + part) * 0.125).T.astype(BF)


def select_body(info, rowid, t0, t1, t2, t3, _, out):
    table = jnp.concatenate([t0[...], t1[...], t2[...], t3[...]], 0)
    shape = (GRID * 4 * SLOTS, RING * GRID * 8)
    r, c = iota(shape, 0), iota(shape, 1)
    tile = ((c // 8) % GRID) * RING + ring_place(info, c // 128)
    hit = (rowid[...] == tile) & ((r // SLOTS) % 4 == c % 4)
    for half in range(2):
        pick = hit & ((c // 4) % 2 == half)
        out[:, half * 512 : half * 512 + 512] = nn(pick.astype(F32).astype(BF), table).astype(BF)


def sum_body(info, rowid, b, z0, z1, z2, z3):
    rows = RING * GRID * 8
    shape = (rows, GRID * 4 * SLOTS)
    r, c = iota(shape, 0), iota(shape, 1)
    target = ((r // 8) % GRID) * RING + ring_place(info, r // 128)
    hit = (rowid[...] == target) & (r % 4 == (c // SLOTS) % 4)
    total = jnp.zeros((rows, D // 2), F32)
    for half in range(2):
        pick = hit & ((r // 4) % 2 == half)
        total += nn(pick.astype(F32).astype(BF), b[:, half * 512 : half * 512 + 512])
    total = total.astype(BF)
    for i, z in enumerate((z0, z1, z2, z3)):
        z[...] = total[i * 128 : i * 128 + 128]


def merge_body(z0, z1, z2, z3, e0, e1, e2, e3, _, out):
    def total(parts):
        return functools.reduce(jnp.add, [part[...].astype(F32) for part in parts])

    out[...] = jnp.concatenate([total((z0, z1, z2, z3)), total((e0, e1, e2, e3))], 1).astype(BF)


def final_body(info, strip_rows, gk, gv, ret, r_in, gk_out, gv_out, w_out):
    half = pl.program_id(0) // 2
    shape = (GRID * 16, TILE)
    r, t = iota(shape, 0), iota(shape, 1)
    hit = strip_target(info, strip_rows, shape, 16) == t
    arrived = r_in[...]
    for part, (grad, out) in enumerate(((gk, gk_out), (gv, gv_out))):
        for f in range(2):
            pick = hit & (r % 16 == half * 4 + 2 * f + part)
            total = grad[f] + tn(pick.astype(F32).astype(BF), arrived)
            if f == 1:
                total = total + ret[part].astype(F32)
            out[f] = total.astype(BF)
    shape = (8, GRID * 16)
    pick = iota(shape, 1) % 16 == 8 + half * 4 + iota(shape, 0)
    w_out[...] = nn(pick.astype(F32).astype(BF), arrived)[:4]


def on_device(
    queries, key_vectors, value_vectors, w_out, rig_tiles, rig_count, strip_rows, cotangent
):
    cam = lax.axis_index("cam")
    tm = lax.axis_index("tm")
    ring = cam % RING
    info = jnp.stack([tm, cam]).astype(jnp.int32)
    strip_rows = strip_rows.T

    q = queries.reshape(2, TILE, D)
    k = key_vectors.reshape(2, TILE, D)
    v = value_vectors.reshape(2, TILE, D)
    cot = cotangent.reshape(2, TILE, D)

    plane = [[p * RING + z for p in range(GRID)] for z in range(RING)]

    def exchange(block):
        return lax.all_to_all(block, "cam", 0, 0, axis_index_groups=plane, tiled=True)

    def along_ring(block, shift):
        route = [
            (p * RING + z, p * RING + (z + shift) % RING)
            for p in range(GRID)
            for z in range(RING)
        ]
        return lax.ppermute(block, "cam", route)

    rigs = lax.dynamic_index_in_dim(rig_tiles.reshape(GRID, RING, 7), ring, 1, keepdims=False)
    counts = lax.dynamic_index_in_dim(rig_count.reshape(GRID, RING), ring, 1, keepdims=False)
    rigs = jnp.where(jnp.arange(7, dtype=jnp.int32) < counts[:, None], rigs, -1)
    rigs = jnp.pad(rigs, ((0, 0), (0, 1)), constant_values=-1)
    rowid = jnp.broadcast_to(rigs[:, None], (GRID, 4, SLOTS)).reshape(-1)

    pair = lambda i, *_: (0, 0, i)
    row = lambda i, *_: (i, 0)
    head = lambda i, *_: (i, 0, 0)
    head4 = lambda i, *_: (i, 0, 0, 0)
    blk = (2, TILE, WIDE)
    stats, sblk = like((PAIRS, 2, WIDE), F32), (2, 2, WIDE)
    heads, hblk = like((PAIRS, 2, TILE, TILE), F32), (2, 2, TILE, TILE)
    act = like((2, TILE, D))

    mine, last = call(
        extract_body,
        (1,),
        [info, strip_rows, (k, None, None), (v, None, None)],
        [(like((GRID * 8, 512)), None, None), (act, None, None)],
        6,
        1 << 27,
        2 << 20,
        scalars=2,
    )
    prev = lax.ppermute(last, "tm", [(i, i + 1) for i in range(3)])
    t0 = exchange(mine.reshape(GRID, 8, 512)).reshape(GRID * 8, 512)
    t1, t2, t3 = [along_ring(t0, s) for s in (1, 2, 3)]

    g, gt = call(
        grad_body,
        (BLOCKS,),
        [(cot, None, None), (w_out, (WIDE, D), row)],
        [(act, blk, pair, NEAR), (like((D, WIDE)), (WIDE, WIDE), row)],
        8,
        1 << 30,
        4 << 20,
        scalars=0,
    )
    m1, l1, o1, cot0 = call(
        local_body,
        (BLOCKS,),
        [
            info,
            (q, blk, pair),
            (k, blk, pair),
            (v, blk, pair),
            (prev, blk, pair),
            (cot, blk, pair),
            (t0, AFTER, None),
        ],
        [
            (stats, sblk, head, NEAR),
            (stats, sblk, head, NEAR),
            (heads, hblk, head4, NEAR),
            (act, blk, pair),
        ],
        8,
        1 << 30,
        4 << 20,
    )

    (sends,) = call(
        select_body,
        (1,),
        [info, (rowid.reshape(-1, 1), None, None, NEAR)]
        + [(t, None, None, NEAR) for t in (t0, t1, t2, t3)]
        + [(m1, AFTER, None)],
        [(like((GRID * 4 * SLOTS, D)), None, None)],
        10,
        1 << 29,
        2 << 20,
    )
    cot1 = lax.ppermute(cot0, "tm", [(t, t ^ 1) for t in range(4)])
    cot2 = lax.ppermute(cot0, "tm", [(t, t ^ 2) for t in range(4)])
    cot3 = lax.ppermute(cot2, "tm", [(t, t ^ 1) for t in range(4)])
    strips = exchange(sends.reshape(GRID, 4 * SLOTS, D)).reshape(GRID, 4, SLOTS, D)

    def block_of(i, info):
        return info[TM] ^ i

    opair = lambda i, info, _: (0, 0, block_of(i, info))
    orow = lambda i, info, _: (block_of(i, info), 0)
    ohead = lambda i, info, _: (block_of(i, info), 0, 0)
    ohead4 = lambda i, info, _: (block_of(i, info), 0, 0, 0)
    gblk = (GRID, 4, SLOTS, WIDE)
    gpair = lambda i, info, _: (0, 0, 0, block_of(i, info))
    back, m, rl, delta, dq, *ots = call(
        strip_body,
        (BLOCKS,),
        [
            info,
            rig_count,
            (q, blk, opair),
            (g, blk, opair, NEAR),
            (gt, (WIDE, WIDE), orow),
            (strips, gblk, gpair, NEAR),
            (m1, sblk, ohead, NEAR),
            (l1, sblk, ohead, NEAR),
            (o1, hblk, ohead4, NEAR),
            (cot3, AFTER, None),
        ],
        [
            (like((GRID, 4, SLOTS, D)), gblk, gpair),
            (stats, sblk, ohead),
            (stats, sblk, ohead),
            (stats, sblk, ohead),
            (heads, hblk, ohead4),
        ]
        + [(like((WIDE, WIDE)), None, None)] * 4,
        10,
        1 << 20,
        1 << 20,
        scalars=2,
    )
    own_ots = ots
    ots = [ots[0]] + [
        lax.ppermute(ots[i], "tm", [(t, t ^ i) for t in range(4)]) for i in (1, 2, 3)
    ]
    b = exchange(back.reshape(GRID, 4 * SLOTS, D)).reshape(GRID * 4 * SLOTS, D)

    piece = (like((GRID * 8, 512)), None, None, NEAR)
    es = call(
        weight_body,
        (1,),
        [info] + [(o, None, None) for o in (cot0, cot1, cot2, cot3, *ots)],
        [piece] * 4,
        12,
        1 << 34,
        6 << 20,
    )

    es = [es[0]] + [along_ring(es[s], -s) for s in (1, 2, 3)]
    zs = call(
        sum_body,
        (1,),
        [info, (rowid.reshape(1, -1), None, None, NEAR), (b, None, None, NEAR)],
        [piece] * 4,
        10,
        1 << 29,
        2 << 20,
    )
    pieces = [zs[0]] + [along_ring(zs[s], -s) for s in (1, 2, 3)]

    gq, gk, gv, ret = call(
        back_body,
        (BLOCKS,),
        [
            info,
            (q, blk, pair),
            (k, blk, pair),
            (v, blk, pair),
            (prev, blk, pair),
            (g, blk, pair),
            (m, sblk, head),
            (rl, sblk, head),
            (delta, sblk, head),
            (dq, hblk, head4),
            (zs[0], AFTER, None),
        ],
        [
            (act, blk, pair),
            (like((2, TILE, D), F32), blk, pair, NEAR),
            (like((2, TILE, D), F32), blk, pair, NEAR),
            (act, blk, pair),
        ],
        14,
        1 << 30,
        8 << 20,
    )
    returned = lax.ppermute(ret, "tm", [(i + 1, i) for i in range(3)])

    (summed,) = call(
        merge_body,
        (1,),
        [(x.reshape(GRID, 8, 512), None, None, NEAR) for x in pieces + es] + [(gq, AFTER, FAR)],
        [(like((GRID, 16, 512)), None, None)],
        6,
        1 << 20,
        1 << 20,
        scalars=0,
    )
    arrived = exchange(summed).reshape(GRID * 16, 512)
    (mixed,) = call(
        mixed_body,
        (2,),
        [info]
        + [(o, None, None) for o in own_ots]
        + [(w_out, (D, 512), lambda i, *_: (0, i)), (summed, AFTER, None)],
        [(act, (2, TILE, 512), pair)],
        8,
        1 << 34,
        4 << 20,
    )

    quarter = (2, TILE, 256)
    grad_k, grad_v, grad_w = call(
        final_body,
        (4,),
        [
            info,
            strip_rows,
            (gk, quarter, pair, NEAR),
            (gv, quarter, pair, NEAR),
            (returned, quarter, pair, NEAR),
            (arrived, (GRID * 16, 256), lambda i, *_: (0, i % 2), NEAR),
        ],
        [
            (act, quarter, pair),
            (act, quarter, pair),
            (like((4, D), F32), (4, 256), lambda i, *_: (0, i)),
        ],
        8,
        1 << 27,
        4 << 20,
        scalars=2,
    )
    whole = (2, 1, TILE, D)
    return (
        mixed.reshape(whole),
        gq.reshape(whole),
        grad_k.reshape(whole),
        grad_v.reshape(whole),
        grad_w,
    )


def solution(mesh):
    block = P("tm", "cam", None, None)
    return jax.shard_map(
        on_device,
        mesh=mesh,
        in_specs=(block, block, block, P(), P(), P(), P(), block),
        out_specs=(block, block, block, block, P(("tm", "cam"), None)),
        check_vma=False,
    )
```

```python
import functools

import jax
import jax.numpy as jnp
from jax import lax
from jax.experimental import pallas as pl
from jax.experimental.pallas import tpu as pltpu
from jax.sharding import PartitionSpec as P

TILE = 128
D = 1024
PAIRS = 8
RING = 4
GRID = 16
SLOTS = 8
NEG = -1e30
BF = jnp.bfloat16
F32 = jnp.float32
MIB = 1 << 20

TM, CAM = range(2)
BLOCKS = 4
WIDE = 2 * TILE
AFTER, NEAR, FAR = "after", "near", "far"


def nt(a, b):
    return lax.dot_general(a, b, (((1,), (1,)), ((), ())), preferred_element_type=F32)


def tn(a, b):
    return lax.dot_general(a, b, (((0,), (0,)), ((), ())), preferred_element_type=F32)


def nn(a, b):
    return jnp.dot(a, b, preferred_element_type=F32)


def iota(shape, dim):
    return lax.broadcasted_iota(jnp.int32, shape, dim)


def call(body, grid, inputs, outputs, limit_mib, flops, nbytes, scalars=1):
    def space(entry):
        return pltpu.VMEM if entry[-1] == NEAR else pltpu.HBM

    def place(entry):
        if not isinstance(entry, tuple):
            return entry
        if entry[1:] == (AFTER, None):
            return entry[0]
        return pltpu.with_memory_space_constraint(entry[0], space(entry))

    def spec(entry):
        shape, block, index = entry[:3]
        if block == AFTER:
            return pl.BlockSpec(memory_space=pl.ANY)
        if block is None:
            zeros = (0,) * len(shape.shape)
            return pl.BlockSpec(shape.shape, lambda *_: zeros)
        return pl.BlockSpec(block, index)

    return pl.pallas_call(
        body,
        grid_spec=pltpu.PrefetchScalarGridSpec(
            num_scalar_prefetch=scalars,
            grid=grid,
            in_specs=[spec(e) for e in inputs[scalars:]],
            out_specs=[spec(e) for e in outputs],
        ),
        out_shape=[space(e)(e[0].shape, e[0].dtype) for e in outputs],
        compiler_params=pltpu.CompilerParams(vmem_limit_bytes=limit_mib * MIB),
        cost_estimate=pl.CostEstimate(flops=flops, bytes_accessed=nbytes, transcendentals=0),
    )(*[place(e) for e in inputs])


def like(shape, dtype=BF):
    return jax.ShapeDtypeStruct(shape, dtype)


def strip_target(info, strip_rows, shape, group):
    s = iota(shape, 0) // group
    target = jnp.zeros(shape, jnp.int32)
    for i in range(GRID):
        target = jnp.where(s == i, strip_rows[i, info[CAM]], target)
    return target


def ring_place(info, back):
    return (info[CAM] + RING - back) % RING


def extract_body(info, strip_rows, k, v, out, last):
    shape = (GRID * 8, 2 * TILE)
    r, c = iota(shape, 0), iota(shape, 1)
    hit = (strip_target(info, strip_rows, shape, 8) == c % TILE) & ((r // 2) % 2 == c // TILE)
    total = jnp.zeros((GRID * 8, D // 2), F32)
    for part, ref in enumerate((k, v)):
        whole = ref[...].reshape(2 * TILE, D)
        for half in range(2):
            pick = hit & (r % 2 == part) & ((r // 4) % 2 == half)
            total += nn(pick.astype(F32).astype(BF), whole[:, half * 512 : half * 512 + 512])
        last[part] = ref[1]
    out[...] = total.astype(BF)


def stacked(block):
    first = iota(block.shape, 1) < 64
    zero = jnp.zeros_like(block)
    return jnp.concatenate([jnp.where(first, block, zero), jnp.where(first, zero, block)], 0)


def own_half(wide):
    return jnp.concatenate([wide[:64, :TILE], wide[64:, TILE:]], 0)


def spread(row):
    return jnp.concatenate(
        [jnp.broadcast_to(row[:, :TILE], (64, TILE)), jnp.broadcast_to(row[:, TILE:], (64, TILE))],
        0,
    )


def units(pairs=2):
    return [(n, slice(n * TILE, n * TILE + TILE), f) for n in range(pairs) for f in range(2)]


def grad_body(cot, w, g_out, gt_out):
    cots = cot[...].reshape(2 * TILE, D)
    g_out[...] = nt(cots, w[...]).astype(BF).reshape(2, TILE, WIDE)
    gt_out[...] = nt(w[...], cots).astype(BF)


def local_body(info, q, k, v, prev, cot, _, m_out, l_out, o_out, cot_out):
    cot_out[...] = cot[...]
    for n, at, f in units(4):
        qs = stacked(q[f, :, at] * jnp.asarray(0.125, BF))
        before_k, before_v = (prev[0, :, at], prev[1, :, at]) if f == 0 else (k[0, :, at], v[0, :, at])
        s1 = nt(k[f, :, at], qs)
        s2 = nt(before_k, qs)
        if f == 0:
            s2 = jnp.where(info[TM] > 0, s2, NEG)
        m = jnp.maximum(jnp.max(s1, 0, keepdims=True), jnp.max(s2, 0, keepdims=True))
        p1 = jnp.exp(s1 - m)
        p2 = jnp.exp(s2 - m)
        m_out[n, f] = m[0]
        l_out[n, f] = jnp.sum(p1, 0) + jnp.sum(p2, 0)
        o_out[n, f] = own_half(tn(v[f, :, at], p1.astype(BF)) + tn(before_v, p2.astype(BF)))


def strip_body(
    info, rig_count, q, g, gt, strips, m1, l1, o1, _,
    back, m_out, rl_out, delta_out, dq_out, *ot_out,
):
    seen = iota((TILE, WIDE), 0) % SLOTS < rig_count[info[CAM]]
    ots = {}
    for n, at, f in units(4):
        qs = stacked(q[f, :, at] * jnp.asarray(0.125, BF))
        gs = stacked(g[f, :, at])
        ks = strips[:, 2 * f, :, at].astype(F32).reshape(TILE, TILE).astype(BF)
        vs = strips[:, 2 * f + 1, :, at].astype(F32).reshape(TILE, TILE).astype(BF)
        s = jnp.where(seen, nt(ks, qs), NEG)
        m_old = m1[n, f : f + 1]
        m = jnp.maximum(m_old, jnp.max(s, 0, keepdims=True))
        p = jnp.exp(s - m)
        shrink = jnp.exp(m_old - m)
        rl = 1.0 / (l1[n, f : f + 1] * shrink + jnp.sum(p, 0, keepdims=True))
        p = p * rl
        pb = p.astype(BF)
        ot = (o1[n, f] * spread(shrink * rl) + own_half(tn(vs, pb))).astype(BF)
        prod = gt[at, f * TILE : f * TILE + TILE].astype(F32) * ot.astype(F32)
        delta = jnp.concatenate(
            [jnp.sum(prod[:64], 0, keepdims=True), jnp.sum(prod[64:], 0, keepdims=True)], 1
        )
        ds = (p * (nt(vs, gs) - delta)).astype(BF)
        back[:, 2 * f, :, at] = nn(ds, qs).reshape(GRID, SLOTS, TILE).astype(BF)
        back[:, 2 * f + 1, :, at] = nn(pb, gs).reshape(GRID, SLOTS, TILE).astype(BF)
        dq_out[n, f] = own_half(tn(ks, ds))
        m_out[n, f] = m[0]
        rl_out[n, f] = rl[0]
        delta_out[n, f] = delta[0]
        ots[n, f] = ot
    sides = [
        jnp.concatenate([jnp.concatenate([ots[n, 0], ots[n, 1]], 1) for n in (i, i + 1)], 0)
        for i in (0, 2)
    ]
    even = info[TM] % 2 == 0
    mine = jnp.where(even, sides[0], sides[1])
    other = jnp.where(even, sides[1], sides[0])
    for i, out in enumerate(ot_out):

        @pl.when(pl.program_id(0) == i // 2)
        def _():
            out[...] = other if i % 2 else mine


def weight_body(info, c0, c1, c2, c3, ot0, ot1, ot2, ot3, e0, e1, e2, e3):
    total = jnp.zeros((WIDE, D), F32)
    for ot, c in ((ot0, c0), (ot1, c1), (ot2, c2), (ot3, c3)):
        total += nn(ot[...], c[...].reshape(WIDE, D))
    total = total.astype(BF)
    shape = (RING * GRID * 8, WIDE)
    r, c = iota(shape, 0), iota(shape, 1)
    hit = c == ((r // 8) % GRID) * 16 + ring_place(info, r // 128) * 4 + r % 4
    out = jnp.zeros((RING * GRID * 8, D // 2), F32)
    for half in range(2):
        pick = hit & ((r // 4) % 2 == half)
        out += nn(pick.astype(F32).astype(BF), total[:, half * 512 : half * 512 + 512])
    out = out.astype(BF)
    for i, e in enumerate((e0, e1, e2, e3)):
        e[...] = out[i * 128 : i * 128 + 128]


def mixed_body(info, ot0, ot1, ot2, ot3, w, _, out):
    total = jnp.zeros((WIDE, 512), F32)
    for i, ot in enumerate((ot0, ot1, ot2, ot3)):
        total += tn(ot[...], w[pl.ds((info[TM] ^ i) * WIDE, WIDE)])
    out[...] = total.astype(BF).reshape(2, TILE, 512)


def block_back(kb, vb, qs, gs, m, rl, delta, hidden=None):
    s = nt(kb, qs)
    if hidden is not None:
        s = jnp.where(hidden, NEG, s)
    p = jnp.exp(s - m) * rl
    ds = (p * (nt(vb, gs) - delta)).astype(BF)
    return nn(ds, qs), nn(p.astype(BF), gs), own_half(tn(kb, ds))


def back_body(
    info, q, k, v, prev, g, m, rl, delta, dq, _, gq_out, gk_out, gv_out, ret_out
):
    hidden = (iota((2 * TILE, WIDE), 0) >= TILE) & (info[TM] == 0)
    for n in range(4):
        at = slice(n * TILE, n * TILE + TILE)
        for f in range(2):
            qs = stacked(q[f, :, at] * jnp.asarray(0.125, BF))
            gs = stacked(g[f, :, at])
            before_k, before_v = (prev[0], prev[1]) if f == 0 else (k[0], v[0])
            keys = jnp.concatenate([k[f, :, at], before_k[:, at]], 0)
            values = jnp.concatenate([v[f, :, at], before_v[:, at]], 0)
            dk, dv, part = block_back(
                keys, values, qs, gs, m[n, f : f + 1], rl[n, f : f + 1], delta[n, f : f + 1],
                hidden if f == 0 else None,
            )
            if f == 0:
                dk0, dv0 = dk[:TILE], dv[:TILE]
                ret_out[0, :, at] = dk[TILE:].astype(BF)
                ret_out[1, :, at] = dv[TILE:].astype(BF)
            else:
                gk_out[1, :, at] = dk[:TILE]
                gv_out[1, :, at] = dv[:TILE]
                gk_out[0, :, at] = dk0 + dk[TILE:]
                gv_out[0, :, at] = dv0 + dv[TILE:]
            gq_out[f, :, at] = ((dq[n, f] + part) * 0.125).T.astype(BF)


def select_body(info, rowid, t0, t1, t2, t3, _, out):
    table = jnp.concatenate([t0[...], t1[...], t2[...], t3[...]], 0)
    shape = (GRID * 4 * SLOTS, RING * GRID * 8)
    r, c = iota(shape, 0), iota(shape, 1)
    tile = ((c // 8) % GRID) * RING + ring_place(info, c // 128)
    hit = (rowid[...] == tile) & ((r // SLOTS) % 4 == c % 4)
    for half in range(2):
        pick = hit & ((c // 4) % 2 == half)
        out[:, half * 512 : half * 512 + 512] = nn(pick.astype(F32).astype(BF), table).astype(BF)


def sum_body(info, rowid, b, z0, z1, z2, z3):
    rows = RING * GRID * 8
    shape = (rows, GRID * 4 * SLOTS)
    r, c = iota(shape, 0), iota(shape, 1)
    target = ((r // 8) % GRID) * RING + ring_place(info, r // 128)
    hit = (rowid[...] == target) & (r % 4 == (c // SLOTS) % 4)
    total = jnp.zeros((rows, D // 2), F32)
    for half in range(2):
        pick = hit & ((r // 4) % 2 == half)
        total += nn(pick.astype(F32).astype(BF), b[:, half * 512 : half * 512 + 512])
    total = total.astype(BF)
    for i, z in enumerate((z0, z1, z2, z3)):
        z[...] = total[i * 128 : i * 128 + 128]


def merge_body(z0, z1, z2, z3, e0, e1, e2, e3, _, out):
    def total(parts):
        return functools.reduce(jnp.add, [part[...].astype(F32) for part in parts])

    out[...] = jnp.concatenate([total((z0, z1, z2, z3)), total((e0, e1, e2, e3))], 1).astype(BF)


def final_body(info, strip_rows, gk, gv, ret, r_in, gk_out, gv_out, w_out):
    half = pl.program_id(0)
    shape = (GRID * 16, TILE)
    r, t = iota(shape, 0), iota(shape, 1)
    hit = strip_target(info, strip_rows, shape, 16) == t
    arrived = r_in[...]
    for part, (grad, out) in enumerate(((gk, gk_out), (gv, gv_out))):
        for f in range(2):
            pick = hit & (r % 16 == half * 4 + 2 * f + part)
            total = grad[f] + tn(pick.astype(F32).astype(BF), arrived)
            if f == 1:
                total = total + ret[part].astype(F32)
            out[f] = total.astype(BF)
    shape = (8, GRID * 16)
    pick = iota(shape, 1) % 16 == 8 + half * 4 + iota(shape, 0)
    w_out[...] = nn(pick.astype(F32).astype(BF), arrived)[:4]


def on_device(
    queries, key_vectors, value_vectors, w_out, rig_tiles, rig_count, strip_rows, cotangent
):
    cam = lax.axis_index("cam")
    tm = lax.axis_index("tm")
    ring = cam % RING
    info = jnp.stack([tm, cam]).astype(jnp.int32)
    strip_rows = pltpu.with_memory_space_constraint(strip_rows.T, pltpu.HBM)
    counts_of = pltpu.with_memory_space_constraint(rig_count, pltpu.HBM)

    q = queries.reshape(2, TILE, D)
    k = key_vectors.reshape(2, TILE, D)
    v = value_vectors.reshape(2, TILE, D)
    cot = cotangent.reshape(2, TILE, D)

    plane = [[p * RING + z for p in range(GRID)] for z in range(RING)]

    def exchange(block):
        return lax.all_to_all(block, "cam", 0, 0, axis_index_groups=plane, tiled=True)

    def along_ring(block, shift):
        route = [
            (p * RING + z, p * RING + (z + shift) % RING)
            for p in range(GRID)
            for z in range(RING)
        ]
        return lax.ppermute(block, "cam", route)

    rigs = lax.dynamic_index_in_dim(rig_tiles.reshape(GRID, RING, 7), ring, 1, keepdims=False)
    counts = lax.dynamic_index_in_dim(rig_count.reshape(GRID, RING), ring, 1, keepdims=False)
    rigs = jnp.where(jnp.arange(7, dtype=jnp.int32) < counts[:, None], rigs, -1)
    rigs = jnp.pad(rigs, ((0, 0), (0, 1)), constant_values=-1)
    rowid = jnp.broadcast_to(rigs[:, None], (GRID, 4, SLOTS)).reshape(-1)

    pair = lambda i, *_: (0, 0, i)
    row = lambda i, *_: (i, 0)
    head = lambda i, *_: (i, 0, 0)
    head4 = lambda i, *_: (i, 0, 0, 0)
    blk = (2, TILE, WIDE)
    wide = (2, TILE, 4 * TILE)
    stats, sblk = like((PAIRS, 2, WIDE), F32), (2, 2, WIDE)
    heads = like((PAIRS, 2, TILE, TILE), F32)
    act = like((2, TILE, D))

    mine, last = call(
        extract_body,
        (1,),
        [info, strip_rows, (k, None, None), (v, None, None)],
        [(like((GRID * 8, 512)), None, None), (act, None, None)],
        6,
        1 << 27,
        2 << 20,
        scalars=2,
    )
    prev = lax.ppermute(last, "tm", [(i, i + 1) for i in range(3)])
    t0 = exchange(mine.reshape(GRID, 8, 512)).reshape(GRID * 8, 512)
    t1, t2, t3 = [along_ring(t0, s) for s in (1, 2, 3)]

    g, gt = call(
        grad_body,
        (BLOCKS,),
        [(cot, None, None), (w_out, (WIDE, D), row)],
        [(act, blk, pair, NEAR), (like((D, WIDE)), (WIDE, WIDE), row)],
        8,
        1 << 30,
        4 << 20,
        scalars=0,
    )
    m1, l1, o1, cot0 = call(
        local_body,
        (2,),
        [
            info,
            (q, wide, pair),
            (k, wide, pair),
            (v, wide, pair),
            (prev, wide, pair, NEAR),
            (cot, wide, pair),
            (t0, AFTER, None),
        ],
        [
            (stats, (4, 2, WIDE), head, NEAR),
            (stats, (4, 2, WIDE), head, NEAR),
            (heads, (4, 2, TILE, TILE), head4, NEAR),
            (act, wide, pair),
        ],
        16,
        1 << 30,
        4 << 20,
    )

    (sends,) = call(
        select_body,
        (1,),
        [info, (rowid.reshape(-1, 1), None, None, NEAR)]
        + [(t, None, None, NEAR) for t in (t0, t1, t2, t3)]
        + [(m1, AFTER, None)],
        [(like((GRID * 4 * SLOTS, D)), None, None)],
        10,
        1 << 29,
        2 << 20,
    )
    cot1 = lax.ppermute(cot0, "tm", [(t, t ^ 1) for t in range(4)])
    cot2 = lax.ppermute(cot0, "tm", [(t, t ^ 2) for t in range(4)])
    cot3 = lax.ppermute(cot2, "tm", [(t, t ^ 1) for t in range(4)])
    strips = exchange(sends.reshape(GRID, 4 * SLOTS, D)).reshape(GRID, 4, SLOTS, D)

    def block_of(i, info):
        return (info[TM] // 2) ^ i

    opair = lambda i, info, _: (0, 0, block_of(i, info))
    orow = lambda i, info, _: (block_of(i, info), 0)
    ohead = lambda i, info, _: (block_of(i, info), 0, 0)
    ohead4 = lambda i, info, _: (block_of(i, info), 0, 0, 0)
    gblk = (GRID, 4, SLOTS, 4 * TILE)
    gpair = lambda i, info, _: (0, 0, 0, block_of(i, info))
    back, m, rl, delta, dq, *ots = call(
        strip_body,
        (2,),
        [
            info,
            counts_of,
            (q, wide, opair),
            (g, wide, opair, NEAR),
            (gt, (4 * TILE, WIDE), orow),
            (strips, gblk, gpair, NEAR),
            (m1, (4, 2, WIDE), ohead, NEAR),
            (l1, (4, 2, WIDE), ohead, NEAR),
            (o1, (4, 2, TILE, TILE), ohead4, NEAR),
            (cot3, AFTER, None),
        ],
        [
            (like((GRID, 4, SLOTS, D)), gblk, gpair),
            (stats, (4, 2, WIDE), ohead),
            (stats, (4, 2, WIDE), ohead),
            (stats, (4, 2, WIDE), ohead),
            (heads, (4, 2, TILE, TILE), ohead4),
        ]
        + [(like((WIDE, WIDE)), None, None)] * 4,
        20,
        1 << 20,
        1 << 20,
        scalars=2,
    )
    own_ots = ots
    ots = [ots[0]] + [
        lax.ppermute(ots[i], "tm", [(t, t ^ i) for t in range(4)]) for i in (1, 2, 3)
    ]
    b = exchange(back.reshape(GRID, 4 * SLOTS, D)).reshape(GRID * 4 * SLOTS, D)

    piece = (like((GRID * 8, 512)), None, None, NEAR)
    es = call(
        weight_body,
        (1,),
        [info] + [(o, None, None) for o in (cot0, cot1, cot2, cot3, *ots)],
        [piece] * 4,
        12,
        1 << 34,
        6 << 20,
    )

    es = [es[0]] + [along_ring(es[s], -s) for s in (1, 2, 3)]
    zs = call(
        sum_body,
        (1,),
        [info, (rowid.reshape(1, -1), None, None, NEAR), (b, None, None, NEAR)],
        [piece] * 4,
        10,
        1 << 29,
        2 << 20,
    )
    pieces = [zs[0]] + [along_ring(zs[s], -s) for s in (1, 2, 3)]

    gq, gk, gv, ret = call(
        back_body,
        (2,),
        [
            info,
            (q, wide, pair),
            (k, wide, pair),
            (v, wide, pair),
            (prev, wide, pair),
            (g, wide, pair),
            (m, (4, 2, WIDE), head),
            (rl, (4, 2, WIDE), head),
            (delta, (4, 2, WIDE), head),
            (dq, (4, 2, TILE, TILE), head4),
            (zs[0], AFTER, None),
        ],
        [
            (act, wide, pair),
            (like((2, TILE, D), F32), wide, pair, NEAR),
            (like((2, TILE, D), F32), wide, pair, NEAR),
            (act, wide, pair),
        ],
        24,
        1 << 30,
        8 << 20,
    )
    returned = lax.ppermute(ret, "tm", [(i + 1, i) for i in range(3)])

    (summed,) = call(
        merge_body,
        (1,),
        [(x.reshape(GRID, 8, 512), None, None, NEAR) for x in pieces + es] + [(gq, AFTER, FAR)],
        [(like((GRID, 16, 512)), None, None)],
        6,
        1 << 20,
        1 << 20,
        scalars=0,
    )
    arrived = exchange(summed).reshape(GRID * 16, 512)
    (mixed,) = call(
        mixed_body,
        (2,),
        [info]
        + [(o, None, None) for o in own_ots]
        + [(w_out, (D, 512), lambda i, *_: (0, i)), (summed, AFTER, None)],
        [(act, (2, TILE, 512), pair)],
        8,
        1 << 34,
        4 << 20,
    )

    grad_k, grad_v, grad_w = call(
        final_body,
        (2,),
        [
            info,
            strip_rows,
            (gk, wide, pair, NEAR),
            (gv, wide, pair, NEAR),
            (returned, wide, pair, NEAR),
            (arrived, None, None, NEAR),
        ],
        [
            (act, wide, pair),
            (act, wide, pair),
            (like((4, D), F32), (4, 512), lambda i, *_: (0, i)),
        ],
        14,
        1 << 27,
        4 << 20,
        scalars=2,
    )
    whole = (2, 1, TILE, D)
    return (
        mixed.reshape(whole),
        gq.reshape(whole),
        grad_k.reshape(whole),
        grad_v.reshape(whole),
        grad_w,
    )


def solution(mesh):
    block = P("tm", "cam", None, None)
    return jax.shard_map(
        on_device,
        mesh=mesh,
        in_specs=(block, block, block, P(), P(), P(), P(), block),
        out_specs=(block, block, block, block, P(("tm", "cam"), None)),
        check_vma=False,
    )
```

```python
import functools

import jax
import jax.numpy as jnp
from jax import lax
from jax.experimental import pallas as pl
from jax.experimental.pallas import tpu as pltpu
from jax.sharding import PartitionSpec as P

TILE = 128
D = 1024
PAIRS = 8
RING = 4
GRID = 16
SLOTS = 8
NEG = -1e30
BF = jnp.bfloat16
F32 = jnp.float32
MIB = 1 << 20

TM, CAM = range(2)
BLOCKS = 4
WIDE = 2 * TILE
AFTER, NEAR, FAR = "after", "near", "far"


def nt(a, b):
    return lax.dot_general(a, b, (((1,), (1,)), ((), ())), preferred_element_type=F32)


def tn(a, b):
    return lax.dot_general(a, b, (((0,), (0,)), ((), ())), preferred_element_type=F32)


def nn(a, b):
    return jnp.dot(a, b, preferred_element_type=F32)


def iota(shape, dim):
    return lax.broadcasted_iota(jnp.int32, shape, dim)


def call(body, grid, inputs, outputs, limit_mib, flops, nbytes, scalars=1):
    def space(entry):
        return pltpu.VMEM if entry[-1] == NEAR else pltpu.HBM

    def place(entry):
        if not isinstance(entry, tuple):
            return entry
        if entry[1:] == (AFTER, None):
            return entry[0]
        return pltpu.with_memory_space_constraint(entry[0], space(entry))

    def spec(entry):
        shape, block, index = entry[:3]
        if block == AFTER:
            return pl.BlockSpec(memory_space=pl.ANY)
        if block is None:
            zeros = (0,) * len(shape.shape)
            return pl.BlockSpec(shape.shape, lambda *_: zeros)
        return pl.BlockSpec(block, index)

    return pl.pallas_call(
        body,
        grid_spec=pltpu.PrefetchScalarGridSpec(
            num_scalar_prefetch=scalars,
            grid=grid,
            in_specs=[spec(e) for e in inputs[scalars:]],
            out_specs=[spec(e) for e in outputs],
        ),
        out_shape=[space(e)(e[0].shape, e[0].dtype) for e in outputs],
        compiler_params=pltpu.CompilerParams(vmem_limit_bytes=limit_mib * MIB),
        cost_estimate=pl.CostEstimate(flops=flops, bytes_accessed=nbytes, transcendentals=0),
    )(*[place(e) for e in inputs])


def like(shape, dtype=BF):
    return jax.ShapeDtypeStruct(shape, dtype)


def strip_target(info, strip_rows, shape, group):
    s = iota(shape, 0) // group
    target = jnp.zeros(shape, jnp.int32)
    for i in range(GRID):
        target = jnp.where(s == i, strip_rows[i, info[CAM]], target)
    return target


def ring_place(info, back):
    return (info[CAM] + RING - back) % RING


def extract_body(info, strip_rows, k, v, out, last):
    shape = (GRID * 8, 2 * TILE)
    r, c = iota(shape, 0), iota(shape, 1)
    hit = (strip_target(info, strip_rows, shape, 8) == c % TILE) & ((r // 2) % 2 == c // TILE)
    total = jnp.zeros((GRID * 8, D // 2), F32)
    for part, ref in enumerate((k, v)):
        whole = ref[...].reshape(2 * TILE, D)
        for half in range(2):
            pick = hit & (r % 2 == part) & ((r // 4) % 2 == half)
            total += nn(pick.astype(F32).astype(BF), whole[:, half * 512 : half * 512 + 512])
        last[part] = ref[1]
    out[...] = total.astype(BF)


def stacked(block):
    first = iota(block.shape, 1) < 64
    zero = jnp.zeros_like(block)
    return jnp.concatenate([jnp.where(first, block, zero), jnp.where(first, zero, block)], 0)


def own_half(wide):
    return jnp.concatenate([wide[:64, :TILE], wide[64:, TILE:]], 0)


def spread(row):
    return jnp.concatenate(
        [jnp.broadcast_to(row[:, :TILE], (64, TILE)), jnp.broadcast_to(row[:, TILE:], (64, TILE))],
        0,
    )


def units(pairs=2):
    return [(n, slice(n * TILE, n * TILE + TILE), f) for n in range(pairs) for f in range(2)]


def grad_body(cot, w, g_out, gt_out):
    cots = cot[...].reshape(2 * TILE, D)
    g_out[...] = nt(cots, w[...]).astype(BF).reshape(2, TILE, WIDE)
    gt_out[...] = nt(w[...], cots).astype(BF)


def local_body(info, q, k, v, prev, cot, _, m_out, l_out, o_out, cot_out):
    cot_out[...] = cot[...]
    for n, at, f in units(4):
        qs = stacked(q[f, :, at] * jnp.asarray(0.125, BF))
        before_k, before_v = (prev[0, :, at], prev[1, :, at]) if f == 0 else (k[0, :, at], v[0, :, at])
        s1 = nt(k[f, :, at], qs)
        s2 = nt(before_k, qs)
        if f == 0:
            s2 = jnp.where(info[TM] > 0, s2, NEG)
        m = jnp.maximum(jnp.max(s1, 0, keepdims=True), jnp.max(s2, 0, keepdims=True))
        p1 = jnp.exp(s1 - m)
        p2 = jnp.exp(s2 - m)
        m_out[n, f] = m[0]
        l_out[n, f] = jnp.sum(p1, 0) + jnp.sum(p2, 0)
        o_out[n, f] = own_half(tn(v[f, :, at], p1.astype(BF)) + tn(before_v, p2.astype(BF)))


def strip_body(
    info, rig_count, q, g, gt, strips, m1, l1, o1, _, __,
    back, m_out, rl_out, delta_out, dq_out, *ot_out,
):
    seen = iota((TILE, WIDE), 0) % SLOTS < rig_count[info[CAM]]
    ots = {}
    for n, at, f in units(4):
        qs = stacked(q[f, :, at] * jnp.asarray(0.125, BF))
        gs = stacked(g[f, :, at])
        ks = strips[:, 2 * f, :, at].astype(F32).reshape(TILE, TILE).astype(BF)
        vs = strips[:, 2 * f + 1, :, at].astype(F32).reshape(TILE, TILE).astype(BF)
        s = jnp.where(seen, nt(ks, qs), NEG)
        m_old = m1[n, f : f + 1]
        m = jnp.maximum(m_old, jnp.max(s, 0, keepdims=True))
        p = jnp.exp(s - m)
        shrink = jnp.exp(m_old - m)
        rl = 1.0 / (l1[n, f : f + 1] * shrink + jnp.sum(p, 0, keepdims=True))
        p = p * rl
        pb = p.astype(BF)
        ot = (o1[n, f] * spread(shrink * rl) + own_half(tn(vs, pb))).astype(BF)
        prod = gt[at, f * TILE : f * TILE + TILE].astype(F32) * ot.astype(F32)
        delta = jnp.concatenate(
            [jnp.sum(prod[:64], 0, keepdims=True), jnp.sum(prod[64:], 0, keepdims=True)], 1
        )
        ds = (p * (nt(vs, gs) - delta)).astype(BF)
        back[:, 2 * f, :, at] = nn(ds, qs).reshape(GRID, SLOTS, TILE).astype(BF)
        back[:, 2 * f + 1, :, at] = nn(pb, gs).reshape(GRID, SLOTS, TILE).astype(BF)
        dq_out[n, f] = own_half(tn(ks, ds))
        m_out[n, f] = m[0]
        rl_out[n, f] = rl[0]
        delta_out[n, f] = delta[0]
        ots[n, f] = ot
    sides = [
        jnp.concatenate([jnp.concatenate([ots[n, 0], ots[n, 1]], 1) for n in (i, i + 1)], 0)
        for i in (0, 2)
    ]
    even = info[TM] % 2 == 0
    mine = jnp.where(even, sides[0], sides[1])
    other = jnp.where(even, sides[1], sides[0])
    for i, out in enumerate(ot_out):

        @pl.when(pl.program_id(0) == i // 2)
        def _():
            out[...] = other if i % 2 else mine


def weight_body(info, c0, c1, c2, c3, ot0, ot1, ot2, ot3, e0, e1, e2, e3):
    total = jnp.zeros((WIDE, D), F32)
    for ot, c in ((ot0, c0), (ot1, c1), (ot2, c2), (ot3, c3)):
        total += nn(ot[...], c[...].reshape(WIDE, D))
    total = total.astype(BF)
    shape = (RING * GRID * 8, WIDE)
    r, c = iota(shape, 0), iota(shape, 1)
    hit = c == ((r // 8) % GRID) * 16 + ring_place(info, r // 128) * 4 + r % 4
    out = jnp.zeros((RING * GRID * 8, D // 2), F32)
    for half in range(2):
        pick = hit & ((r // 4) % 2 == half)
        out += nn(pick.astype(F32).astype(BF), total[:, half * 512 : half * 512 + 512])
    out = out.astype(BF)
    for i, e in enumerate((e0, e1, e2, e3)):
        e[...] = out[i * 128 : i * 128 + 128]


def mixed_body(info, ot0, ot1, ot2, ot3, w, _, out):
    total = jnp.zeros((WIDE, 512), F32)
    for i, ot in enumerate((ot0, ot1, ot2, ot3)):
        total += tn(ot[...], w[pl.ds((info[TM] ^ i) * WIDE, WIDE)])
    out[...] = total.astype(BF).reshape(2, TILE, 512)


def block_back(kb, vb, qs, gs, m, rl, delta, hidden=None):
    s = nt(kb, qs)
    if hidden is not None:
        s = jnp.where(hidden, NEG, s)
    p = jnp.exp(s - m) * rl
    ds = (p * (nt(vb, gs) - delta)).astype(BF)
    return nn(ds, qs), nn(p.astype(BF), gs), own_half(tn(kb, ds))


def back_body(
    info, q, k, v, prev, g, m, rl, delta, dq, _, gq_out, gk_out, gv_out, ret_out
):
    hidden = (iota((2 * TILE, WIDE), 0) >= TILE) & (info[TM] == 0)
    for n in range(4):
        at = slice(n * TILE, n * TILE + TILE)
        for f in range(2):
            qs = stacked(q[f, :, at] * jnp.asarray(0.125, BF))
            gs = stacked(g[f, :, at])
            before_k, before_v = (prev[0], prev[1]) if f == 0 else (k[0], v[0])
            keys = jnp.concatenate([k[f, :, at], before_k[:, at]], 0)
            values = jnp.concatenate([v[f, :, at], before_v[:, at]], 0)
            dk, dv, part = block_back(
                keys, values, qs, gs, m[n, f : f + 1], rl[n, f : f + 1], delta[n, f : f + 1],
                hidden if f == 0 else None,
            )
            if f == 0:
                dk0, dv0 = dk[:TILE], dv[:TILE]
                ret_out[0, :, at] = dk[TILE:].astype(BF)
                ret_out[1, :, at] = dv[TILE:].astype(BF)
            else:
                gk_out[1, :, at] = dk[:TILE]
                gv_out[1, :, at] = dv[:TILE]
                gk_out[0, :, at] = dk0 + dk[TILE:]
                gv_out[0, :, at] = dv0 + dv[TILE:]
            gq_out[f, :, at] = ((dq[n, f] + part) * 0.125).T.astype(BF)


def select_body(info, rowid, t0, t1, t2, t3, _, out):
    table = jnp.concatenate([t0[...], t1[...], t2[...], t3[...]], 0)
    shape = (GRID * 4 * SLOTS, RING * GRID * 8)
    r, c = iota(shape, 0), iota(shape, 1)
    tile = ((c // 8) % GRID) * RING + ring_place(info, c // 128)
    hit = (rowid[...] == tile) & ((r // SLOTS) % 4 == c % 4)
    for half in range(2):
        pick = hit & ((c // 4) % 2 == half)
        out[:, half * 512 : half * 512 + 512] = nn(pick.astype(F32).astype(BF), table).astype(BF)


def sum_body(info, rowid, b, z0, z1, z2, z3):
    rows = RING * GRID * 8
    shape = (rows, GRID * 4 * SLOTS)
    r, c = iota(shape, 0), iota(shape, 1)
    target = ((r // 8) % GRID) * RING + ring_place(info, r // 128)
    hit = (rowid[...] == target) & (r % 4 == (c // SLOTS) % 4)
    total = jnp.zeros((rows, D // 2), F32)
    for half in range(2):
        pick = hit & ((r // 4) % 2 == half)
        total += nn(pick.astype(F32).astype(BF), b[:, half * 512 : half * 512 + 512])
    total = total.astype(BF)
    for i, z in enumerate((z0, z1, z2, z3)):
        z[...] = total[i * 128 : i * 128 + 128]


def merge_body(z0, z1, z2, z3, e0, e1, e2, e3, _, out):
    def total(parts):
        return functools.reduce(jnp.add, [part[...].astype(F32) for part in parts])

    out[...] = jnp.concatenate([total((z0, z1, z2, z3)), total((e0, e1, e2, e3))], 1).astype(BF)


def final_body(info, strip_rows, gk, gv, ret, r_in, gk_out, gv_out, w_out):
    half = pl.program_id(0)
    shape = (GRID * 16, TILE)
    r, t = iota(shape, 0), iota(shape, 1)
    hit = strip_target(info, strip_rows, shape, 16) == t
    arrived = r_in[...]
    for part, (grad, out) in enumerate(((gk, gk_out), (gv, gv_out))):
        for f in range(2):
            pick = hit & (r % 16 == half * 4 + 2 * f + part)
            total = grad[f] + tn(pick.astype(F32).astype(BF), arrived)
            if f == 1:
                total = total + ret[part].astype(F32)
            out[f] = total.astype(BF)
    shape = (8, GRID * 16)
    pick = iota(shape, 1) % 16 == 8 + half * 4 + iota(shape, 0)
    w_out[...] = nn(pick.astype(F32).astype(BF), arrived)[:4]


def on_device(
    queries, key_vectors, value_vectors, w_out, rig_tiles, rig_count, strip_rows, cotangent
):
    cam = lax.axis_index("cam")
    tm = lax.axis_index("tm")
    ring = cam % RING
    info = jnp.stack([tm, cam]).astype(jnp.int32)
    strip_rows = pltpu.with_memory_space_constraint(strip_rows.T, pltpu.HBM)
    counts_of = pltpu.with_memory_space_constraint(rig_count, pltpu.HBM)

    q = queries.reshape(2, TILE, D)
    k = key_vectors.reshape(2, TILE, D)
    v = value_vectors.reshape(2, TILE, D)
    cot = cotangent.reshape(2, TILE, D)

    plane = [[p * RING + z for p in range(GRID)] for z in range(RING)]

    def exchange(block):
        return lax.all_to_all(block, "cam", 0, 0, axis_index_groups=plane, tiled=True)

    def along_ring(block, shift):
        route = [
            (p * RING + z, p * RING + (z + shift) % RING)
            for p in range(GRID)
            for z in range(RING)
        ]
        return lax.ppermute(block, "cam", route)

    rigs = lax.dynamic_index_in_dim(rig_tiles.reshape(GRID, RING, 7), ring, 1, keepdims=False)
    counts = lax.dynamic_index_in_dim(rig_count.reshape(GRID, RING), ring, 1, keepdims=False)
    rigs = jnp.where(jnp.arange(7, dtype=jnp.int32) < counts[:, None], rigs, -1)
    rigs = jnp.pad(rigs, ((0, 0), (0, 1)), constant_values=-1)
    rowid = jnp.broadcast_to(rigs[:, None], (GRID, 4, SLOTS)).reshape(-1)

    pair = lambda i, *_: (0, 0, i)
    row = lambda i, *_: (i, 0)
    head = lambda i, *_: (i, 0, 0)
    head4 = lambda i, *_: (i, 0, 0, 0)
    blk = (2, TILE, WIDE)
    wide = (2, TILE, 4 * TILE)
    stats, sblk = like((PAIRS, 2, WIDE), F32), (2, 2, WIDE)
    heads = like((PAIRS, 2, TILE, TILE), F32)
    act = like((2, TILE, D))

    mine, last = call(
        extract_body,
        (1,),
        [info, strip_rows, (k, None, None), (v, None, None)],
        [(like((GRID * 8, 512)), None, None), (act, None, None)],
        6,
        1 << 27,
        2 << 20,
        scalars=2,
    )
    prev = lax.ppermute(last, "tm", [(i, i + 1) for i in range(3)])
    t0 = exchange(mine.reshape(GRID, 8, 512)).reshape(GRID * 8, 512)
    t1, t2, t3 = [along_ring(t0, s) for s in (1, 2, 3)]

    g, gt = call(
        grad_body,
        (BLOCKS,),
        [(cot, None, None), (w_out, (WIDE, D), row)],
        [(act, blk, pair, NEAR), (like((D, WIDE)), (WIDE, WIDE), row)],
        8,
        1 << 30,
        4 << 20,
        scalars=0,
    )
    m1, l1, o1, cot0 = call(
        local_body,
        (2,),
        [
            info,
            (q, wide, pair),
            (k, wide, pair),
            (v, wide, pair),
            (prev, wide, pair, NEAR),
            (cot, wide, pair),
            (t0, AFTER, None),
        ],
        [
            (stats, (4, 2, WIDE), head, NEAR),
            (stats, (4, 2, WIDE), head, NEAR),
            (heads, (4, 2, TILE, TILE), head4, NEAR),
            (act, wide, pair),
        ],
        16,
        1 << 30,
        4 << 20,
    )

    (sends,) = call(
        select_body,
        (1,),
        [info, (rowid.reshape(-1, 1), None, None, NEAR)]
        + [(t, None, None, NEAR) for t in (t0, t1, t2, t3)]
        + [(m1, AFTER, None)],
        [(like((GRID * 4 * SLOTS, D)), None, None)],
        10,
        1 << 29,
        2 << 20,
    )
    cot1 = lax.ppermute(cot0, "tm", [(t, t ^ 1) for t in range(4)])
    cot2 = lax.ppermute(cot0, "tm", [(t, t ^ 2) for t in range(4)])
    cot3 = lax.ppermute(cot2, "tm", [(t, t ^ 1) for t in range(4)])
    strips = exchange(sends.reshape(GRID, 4 * SLOTS, D)).reshape(GRID, 4, SLOTS, D)

    def block_of(i, info):
        return (info[TM] // 2) ^ i

    opair = lambda i, info, _: (0, 0, block_of(i, info))
    orow = lambda i, info, _: (block_of(i, info), 0)
    ohead = lambda i, info, _: (block_of(i, info), 0, 0)
    ohead4 = lambda i, info, _: (block_of(i, info), 0, 0, 0)
    gblk = (GRID, 4, SLOTS, 4 * TILE)
    gpair = lambda i, info, _: (0, 0, 0, block_of(i, info))
    back, m, rl, delta, dq, *ots = call(
        strip_body,
        (2,),
        [
            info,
            counts_of,
            (q, wide, opair),
            (g, wide, opair, NEAR),
            (gt, (4 * TILE, WIDE), orow),
            (strips, gblk, gpair, NEAR),
            (m1, (4, 2, WIDE), ohead, NEAR),
            (l1, (4, 2, WIDE), ohead, NEAR),
            (o1, (4, 2, TILE, TILE), ohead4, NEAR),
            (cot3, AFTER, None),
            (cot1, AFTER, None),
        ],
        [
            (like((GRID, 4, SLOTS, D)), gblk, gpair),
            (stats, (4, 2, WIDE), ohead),
            (stats, (4, 2, WIDE), ohead),
            (stats, (4, 2, WIDE), ohead),
            (heads, (4, 2, TILE, TILE), ohead4),
        ]
        + [(like((WIDE, WIDE)), None, None)] * 4,
        20,
        1 << 20,
        1 << 20,
        scalars=2,
    )
    own_ots = ots
    ots = [ots[0]] + [
        lax.ppermute(ots[i], "tm", [(t, t ^ i) for t in range(4)]) for i in (1, 2, 3)
    ]
    b = exchange(back.reshape(GRID, 4 * SLOTS, D)).reshape(GRID * 4 * SLOTS, D)

    piece = (like((GRID * 8, 512)), None, None, NEAR)
    es = call(
        weight_body,
        (1,),
        [info] + [(o, None, None) for o in (cot0, cot1, cot2, cot3, *ots)],
        [piece] * 4,
        12,
        1 << 34,
        6 << 20,
    )

    es = [es[0]] + [along_ring(es[s], -s) for s in (1, 2, 3)]
    zs = call(
        sum_body,
        (1,),
        [info, (rowid.reshape(1, -1), None, None, NEAR), (b, None, None, NEAR)],
        [piece] * 4,
        10,
        1 << 29,
        2 << 20,
    )
    pieces = [zs[0]] + [along_ring(zs[s], -s) for s in (1, 2, 3)]

    gq, gk, gv, ret = call(
        back_body,
        (2,),
        [
            info,
            (q, wide, pair),
            (k, wide, pair),
            (v, wide, pair),
            (prev, wide, pair),
            (g, wide, pair),
            (m, (4, 2, WIDE), head),
            (rl, (4, 2, WIDE), head),
            (delta, (4, 2, WIDE), head),
            (dq, (4, 2, TILE, TILE), head4),
            (zs[0], AFTER, None),
        ],
        [
            (act, wide, pair),
            (like((2, TILE, D), F32), wide, pair, NEAR),
            (like((2, TILE, D), F32), wide, pair, NEAR),
            (act, wide, pair),
        ],
        24,
        1 << 30,
        8 << 20,
    )
    returned = lax.ppermute(ret, "tm", [(i + 1, i) for i in range(3)])

    (summed,) = call(
        merge_body,
        (1,),
        [(x.reshape(GRID, 8, 512), None, None, NEAR) for x in pieces + es] + [(gq, AFTER, FAR)],
        [(like((GRID, 16, 512)), None, None)],
        6,
        1 << 20,
        1 << 20,
        scalars=0,
    )
    arrived = exchange(summed).reshape(GRID * 16, 512)
    (mixed,) = call(
        mixed_body,
        (2,),
        [info]
        + [(o, None, None) for o in own_ots]
        + [(w_out, (D, 512), lambda i, *_: (0, i)), (summed, AFTER, None)],
        [(act, (2, TILE, 512), pair)],
        8,
        1 << 34,
        4 << 20,
    )

    grad_k, grad_v, grad_w = call(
        final_body,
        (2,),
        [
            info,
            strip_rows,
            (gk, wide, pair, NEAR),
            (gv, wide, pair, NEAR),
            (returned, wide, pair, NEAR),
            (arrived, None, None, NEAR),
        ],
        [
            (act, wide, pair),
            (act, wide, pair),
            (like((4, D), F32), (4, 512), lambda i, *_: (0, i)),
        ],
        14,
        1 << 27,
        4 << 20,
        scalars=2,
    )
    whole = (2, 1, TILE, D)
    return (
        mixed.reshape(whole),
        gq.reshape(whole),
        grad_k.reshape(whole),
        grad_v.reshape(whole),
        grad_w,
    )


def solution(mesh):
    block = P("tm", "cam", None, None)
    return jax.shard_map(
        on_device,
        mesh=mesh,
        in_specs=(block, block, block, P(), P(), P(), P(), block),
        out_specs=(block, block, block, block, P(("tm", "cam"), None)),
        check_vma=False,
    )
```
